128 devices in a mesh: row: 4 (over z_hi, core), col: 32 (over z_lo, x, y).
Axes of the slice: x: 4, y: 4, z: 4 (z_hi: 2, z_lo: 2; z = z_hi * 2 + z_lo), core: 2. Of those that a mesh axis runs over, the one named last changes fastest.
Arguments:
- tokens: bfloat16 [512, 12288], P('col', 'row'), may hold values from -6 to 6
- cotangent: bfloat16 [512, 12288], P('col', 'row'), may hold values from -6 to 6
- gate_weight: bfloat16 [12288, 24576], P('row', 'col'), may hold values from -0.109375 to 0.109375
- up_weight: bfloat16 [12288, 24576], P('row', 'col'), may hold values from -0.109375 to 0.109375
- down_weight: bfloat16 [24576, 12288], P('col', 'row'), may hold values from -0.078125 to 0.078125
- kept: int32 [3, 96, 192], P(None, 'row', 'col'), may hold values from 0 to 1, as said below
- regrown: int32 [3, 96, 192], P(None, 'row', 'col'), may hold values from 0 to 1, as said below
Outputs:
- output: bfloat16 [512, 12288], P('col', 'row')
- input_grad: bfloat16 [512, 12288], P('col', 'row')
- grad_blocks: bfloat16 [3, 4, 32, 36, 128, 128], P(None, 'row', 'col')
The draws below stay inside these ranges and needn't reach their ends.
Inputs may be any that keep to these rules, and one draw needn't show every extreme that they name: kept and regrown never both 1. Within each grid row and weight exactly 1152 blocks are active; each tile of 24 x 6 blocks holds between 18 and 72 active blocks, and one tile of every grid row and weight holds exactly 72. `regrown`: same layout as kept.
All inputs are finite; a program needn't handle non-finite values.
Results may differ from the reference program's by a relative error of at most 0.0049.
Values may be sent and summed in bfloat16 or wider, within the bound.
No kernel may reach another device: no remote copies, remote signals or barrier semaphores. Data moves between devices by JAX's collectives and lax.ppermute only.
A program may use at most 128 MiB of HBM per device.

```python
import jax
import jax.numpy as jnp

D = 12288
FFW = 24576
BLOCK = 128
TOKENS = 512
DB = 96
FB = 192
BR = 24
BC = 6
OWN = 36
ACT_ROW = 1152
N_COL = 32


def mask_pair(key):
    n_rows = DB // BR
    n_cols = FB // BC
    tile_size = BR * BC
    groups = 3 * n_rows
    key_perm, key_gap, key_place, key_regrow = jax.random.split(key, 4)
    index = jnp.arange(n_cols)
    base = jnp.full((n_cols,), OWN, jnp.int32)
    base = base.at[0].set(2 * OWN).at[1].set(OWN // 2).at[2].set(OWN // 2)
    pair_count = (n_cols - 3) // 2
    pair_id = jnp.clip((index - 3) // 2, 0, max(pair_count - 1, 0))
    in_pair = (index >= 3) & ((index - 3) // 2 < pair_count)
    sign_of = jnp.where((index - 3) % 2 == 0, 1, -1)
    gaps = jax.random.randint(key_gap, (groups, max(pair_count, 1)), 0, OWN // 2 + 1)
    shifted = jnp.where(in_pair[None, :], sign_of[None, :] * gaps[:, pair_id], 0)
    pattern = base[None, :] + shifted
    orders = jax.vmap(lambda k: jax.random.permutation(k, n_cols))(jax.random.split(key_perm, groups))
    counts = jnp.take_along_axis(pattern, orders, axis=1)
    place_keys = jax.random.split(key_place, groups * n_cols)
    ranks = jax.vmap(lambda k: jnp.argsort(jax.random.permutation(k, tile_size)))(place_keys)
    active = ranks < counts.reshape(-1)[:, None]
    active = active.reshape(3, n_rows, n_cols, BR, BC).transpose(0, 1, 3, 2, 4).reshape(3, DB, FB)
    regrow = jax.random.randint(key_regrow, (3, DB, FB), 0, 4) == 0
    kept_out = (active & ~regrow).astype(jnp.int32)
    grown_out = (active & regrow).astype(jnp.int32)
    return (kept_out, grown_out)


def draw_kept(key, part):
    return mask_pair(key)[0]


def draw_regrown(key, part):
    return mask_pair(key)[1]


def levels(key, dims, shards, low, top_value):
    def one(dim, shards_of):
        heights = jax.random.uniform(jax.random.fold_in(jax.random.fold_in(key, 6), dim), (shards_of,), jnp.float32, low / len(shards), top_value / len(shards))
        return jnp.repeat(jnp.exp(heights), dims[dim] // shards_of).reshape((-1,) + (1,) * (len(dims) - dim - 1))

    factor_of = one(*shards[0])
    for cut in shards[1:]:
        factor_of = factor_of * one(*cut)
    return factor_of


def bell_draw(stream_key, extent, spread, reach, cuts=(), kind=jnp.bfloat16):
    result = spread * jax.random.normal(stream_key, extent, jnp.float32)
    if cuts:
        result = result * levels(stream_key, extent, cuts, -0.22, 0.18)
    return jnp.clip(result, -reach, reach).astype(kind)


def setup_inputs(seed: int = 0) -> dict:
    key_list = jax.random.split(jax.random.key(seed), 8)
    tokens = bell_draw(key_list[0], (TOKENS, D), 1.0, 6.0, ((0, 32), (1, 4)))
    cotangent = bell_draw(key_list[1], (TOKENS, D), 1.0, 6.0, ((0, 32), (1, 4)))
    gate_weight = bell_draw(key_list[2], (D, FFW), (D // 4) ** -0.5, 0.109375, ((0, 4), (1, 32)))
    up_weight = bell_draw(key_list[3], (D, FFW), (D // 4) ** -0.5, 0.109375, ((0, 4), (1, 32)))
    down_weight = bell_draw(key_list[4], (FFW, D), (FFW // 4) ** -0.5, 0.078125, ((0, 32), (1, 4)))
    kept = draw_kept(jax.random.fold_in(key_list[7], 71), 0)
    regrown = draw_regrown(jax.random.fold_in(key_list[7], 71), 0)
    return dict(tokens=tokens, cotangent=cotangent, gate_weight=gate_weight, up_weight=up_weight, down_weight=down_weight, kept=kept, regrown=regrown)


def mask_rows(weight, keep):
    rows, cols = keep.shape
    shaped = weight.reshape(rows, BLOCK, cols, BLOCK) * keep[:, None, :, None]
    return shaped.reshape(weight.shape)


def pick_blocks(grad_tiles, active):
    n_rows = DB // BR
    n_cols = FB // BC
    tile_size = BR * BC
    ordered = active.reshape(n_rows, BR, n_cols, BC).transpose(0, 2, 1, 3).reshape(n_rows, n_cols * tile_size)
    places = jnp.argsort(1 - ordered, axis=1, stable=True)[:, :ACT_ROW].astype(jnp.int32)
    tile_at = places // tile_size
    within = places % tile_size
    block_row = jnp.arange(n_rows, dtype=jnp.int32)[:, None] * BR + within // BC
    block_col = tile_at * BC + within % BC
    chosen = grad_tiles[block_row, block_col]
    chosen = chosen.reshape(n_rows, OWN, N_COL, BLOCK, BLOCK).transpose(0, 2, 1, 3, 4)
    return chosen


def reference(tokens, cotangent, gate_weight, up_weight, down_weight, kept, regrown):
    keep = kept.astype(jnp.bfloat16)
    wg = mask_rows(gate_weight, keep[0])
    wu = mask_rows(up_weight, keep[1])
    wd = mask_rows(down_weight, keep[2].T)
    gate = jnp.dot(tokens, wg, preferred_element_type=jnp.float32)
    up = jnp.dot(tokens, wu, preferred_element_type=jnp.float32)
    sig = jax.nn.sigmoid(gate)
    act = gate * sig
    hidden = (act * up).astype(jnp.bfloat16)
    output = jnp.dot(hidden, wd, preferred_element_type=jnp.float32).astype(jnp.bfloat16)
    hidden_grad = jnp.dot(cotangent, wd.T, preferred_element_type=jnp.float32)
    gate_grad = (hidden_grad * up * sig * (1.0 + gate * (1.0 - sig))).astype(jnp.bfloat16)
    up_grad = (hidden_grad * act).astype(jnp.bfloat16)
    input_grad = (jnp.dot(gate_grad, wg.T, preferred_element_type=jnp.float32)
                  + jnp.dot(up_grad, wu.T, preferred_element_type=jnp.float32)).astype(jnp.bfloat16)
    factor = float(TOKENS) ** -0.5
    active = kept + regrown
    gathered = []
    grad_g = (jnp.dot(tokens.T, gate_grad, preferred_element_type=jnp.float32) * factor).astype(jnp.bfloat16)
    gathered.append(pick_blocks(grad_g.reshape(DB, BLOCK, FB, BLOCK).transpose(0, 2, 1, 3), active[0]))
    grad_u = (jnp.dot(tokens.T, up_grad, preferred_element_type=jnp.float32) * factor).astype(jnp.bfloat16)
    gathered.append(pick_blocks(grad_u.reshape(DB, BLOCK, FB, BLOCK).transpose(0, 2, 1, 3), active[1]))
    grad_d = (jnp.dot(hidden.T, cotangent, preferred_element_type=jnp.float32) * factor).astype(jnp.bfloat16)
    gathered.append(pick_blocks(grad_d.reshape(FB, BLOCK, DB, BLOCK).transpose(2, 0, 1, 3), active[2]))
    grad_blocks = jnp.stack(gathered, 0)
    return output, input_grad, grad_blocks
```

```python
import jax
import jax.numpy as jnp
from jax import lax
from jax.experimental import pallas as pl
from jax.experimental.pallas import tpu as pltpu
from jax.sharding import PartitionSpec as P

BLOCK = 128
MAIN = 7
EXTRA = 2
LANES = 128
BF = jnp.bfloat16
F32 = jnp.float32


def mask_rows(weight, keep):
    rows, cols = keep.shape
    shaped = weight.reshape(rows, BLOCK, cols, BLOCK) * keep[:, None, :, None]
    return shaped.reshape(weight.shape)


def contract_last(left, right):
    return lax.dot_general(left, right, (((1,), (1,)), ((), ())), preferred_element_type=F32)


def gather_rows(part, ncol):
    copies = jnp.broadcast_to(part[None], (ncol,) + part.shape).reshape(ncol * part.shape[0], part.shape[1])
    return lax.all_to_all(copies, "col", 0, 0, tiled=True)


def scatter_sum(partial, ncol):
    rows = partial.shape[0] // ncol
    got = lax.all_to_all(partial.astype(BF), "col", 0, 0, tiled=True)
    return jnp.sum(got.reshape(ncol, rows, -1).astype(F32), axis=0).astype(BF)


def row_sum(value, core):
    half = value.shape[0] // 2
    keep = lax.dynamic_slice_in_dim(value, core * half, half, 0)
    send = lax.dynamic_slice_in_dim(value, (1 - core) * half, half, 0)
    pair = [(0, 1), (1, 0), (2, 3), (3, 2)]
    far = [(0, 2), (1, 3), (2, 0), (3, 1)]
    mine = keep + lax.ppermute(send, "row", pair)
    mine = mine + lax.ppermute(mine.astype(BF), "row", far).astype(F32)
    other = lax.ppermute(mine, "row", pair)
    first = jnp.where(core == 0, mine, other)
    second = jnp.where(core == 0, other, mine)
    return jnp.concatenate([first, second], axis=0)


def dot_rows(left, right):
    return lax.dot_general(left, right, (((0,), (0,)), ((), ())), preferred_element_type=F32)


def pack_kernel(factor, brows, bcols, group, where_ref, x_ref, gg_ref, ug_ref, hid_ref, dy_ref, main_ref, extra_ref):
    cut = main_ref.shape[0]
    wide = group * BLOCK

    def store(which, d, f, block):
        at = where_ref[which * brows * bcols + d * bcols + f]

        @pl.when((at >= 0) & (at < cut))
        def _():
            main_ref[at] = block

        @pl.when(at >= cut)
        def _():
            extra_ref[at - cut] = block

    def step(i, carry):
        lanes = pl.ds(pl.multiple_of(i * wide, wide), wide)
        x = x_ref[:, lanes]
        dy = dy_ref[:, lanes]
        for which, grad_ref in ((0, gg_ref), (1, ug_ref)):
            tile = (dot_rows(x, grad_ref[...]) * factor).astype(BF)
            for u in range(group):
                for f in range(bcols):
                    store(which, i * group + u, f, tile[u * BLOCK:(u + 1) * BLOCK, f * BLOCK:(f + 1) * BLOCK])
        tile = (dot_rows(hid_ref[...], dy) * factor).astype(BF)
        for u in range(group):
            for f in range(bcols):
                store(2, i * group + u, f, tile[f * BLOCK:(f + 1) * BLOCK, u * BLOCK:(u + 1) * BLOCK])
        return carry

    lax.fori_loop(0, brows // group, step, 0)


def pack_grads(where, x_all, gate_grad, up_grad, hidden, dy_all, factor, brows, bcols, ncol):
    import functools

    vmem = pl.BlockSpec(memory_space=pltpu.VMEM)
    tokens = x_all.shape[0]
    feat = brows * BLOCK
    return pl.pallas_call(
        functools.partial(pack_kernel, factor, brows, bcols, 4),
        out_shape=(
            jax.ShapeDtypeStruct((ncol * MAIN, BLOCK, BLOCK), BF),
            jax.ShapeDtypeStruct((ncol * EXTRA, BLOCK, BLOCK), BF),
        ),
        in_specs=[pl.BlockSpec(memory_space=pltpu.SMEM)] + [vmem] * 5,
        out_specs=(vmem, vmem),
        compiler_params=pltpu.CompilerParams(vmem_limit_bytes=48 * 2**20),
        cost_estimate=pl.CostEstimate(flops=6 * tokens * feat * bcols * BLOCK, bytes_accessed=16 * 2**20, transcendentals=0),
    )(where, x_all, gate_grad, up_grad, hidden, dy_all)


def pick_kernel(count, from_ref, got_ref, out_ref):
    def step(i, carry):
        out_ref[i] = got_ref[from_ref[i]]
        return carry

    lax.fori_loop(0, count, step, 0, unroll=4)


def pick_blocks(source, got):
    import functools

    vmem = pl.BlockSpec(memory_space=pltpu.VMEM)
    count = source.shape[0]
    return pl.pallas_call(
        functools.partial(pick_kernel, count),
        out_shape=jax.ShapeDtypeStruct((count, BLOCK, BLOCK), BF),
        in_specs=[pl.BlockSpec(memory_space=pltpu.SMEM), vmem],
        out_specs=vmem,
        compiler_params=pltpu.CompilerParams(vmem_limit_bytes=32 * 2**20),
        cost_estimate=pl.CostEstimate(flops=0, bytes_accessed=12 * 2**20, transcendentals=0),
    )(source, got)


def pair_counts(counts, offsets, ncol):
    owners = jnp.arange(ncol, dtype=jnp.int32)
    first = (owners[None, None, :] - offsets[:, :, None]) % ncol
    return (counts[:, :, None] - first + ncol - 1) // ncol


def send_places(active, counts, offsets, pairs, place, ncol):
    flat = active.reshape(3, -1)
    local = jnp.cumsum(flat, axis=1) - 1
    mine = offsets[:, place][:, None]
    owner = (mine + local) % ncol
    ahead = jnp.cumsum(pairs, axis=0) - pairs
    ahead = ahead[:, place]
    before = jnp.sum(jnp.where(owner[:, :, None] == jnp.arange(ncol)[None, None, :], ahead[:, None, :], 0), axis=2)
    slot = before + local // ncol
    at = jnp.where(slot < MAIN, owner * MAIN + slot, ncol * MAIN + owner * EXTRA + slot - MAIN)
    return jnp.where(flat > 0, at, -1).reshape(-1).astype(jnp.int32)


def pick_places(offsets, pairs, place, own, ncol):
    wanted = jnp.arange(own, dtype=jnp.int32)[None, :] * ncol + place
    source = jnp.sum((offsets[:, None, :] <= wanted[:, :, None]).astype(jnp.int32), axis=2) - 1
    ahead = (jnp.cumsum(pairs, axis=0) - pairs)[:, :, place]
    here = source[:, :, None] == jnp.arange(ncol)[None, None, :]
    start = jnp.sum(jnp.where(here, offsets[:, None, :], 0), axis=2)
    before = jnp.sum(jnp.where(here, ahead[:, None, :], 0), axis=2)
    slot = before + (wanted - start) // ncol
    at = jnp.where(slot < MAIN, source * MAIN + slot, ncol * MAIN + source * EXTRA + slot - MAIN)
    return at.reshape(-1).astype(jnp.int32)


def shards(tokens, cotangent, gate_weight, up_weight, down_weight, kept, regrown):
    keep = kept.astype(BF)
    feat, hid = gate_weight.shape
    brows, bcols = kept.shape[1], kept.shape[2]
    ncol = lax.axis_size("col")
    place = lax.axis_index("col")
    core = lax.axis_index("row") % 2
    own = brows * bcols // 4
    active = kept + regrown
    tally = jnp.sum(active, axis=(1, 2)).astype(BF)
    note = jnp.zeros((tokens.shape[0], LANES), BF).at[0, :3].set(tally)
    x_wide = gather_rows(jnp.concatenate([tokens, note], axis=1), ncol)
    dy_all = gather_rows(cotangent, ncol)
    both = jnp.concatenate([mask_rows(gate_weight, keep[0]), mask_rows(up_weight, keep[1])], axis=1)
    wd = mask_rows(down_weight, keep[2].T)
    x_all = x_wide[:, :feat]
    counts = x_wide.reshape(ncol, -1, feat + LANES)[:, 0, feat:feat + 3].astype(jnp.int32).T
    offsets = jnp.cumsum(counts, axis=1) - counts
    pairs = pair_counts(counts, offsets, ncol)
    need = jnp.max(jnp.sum(pairs, axis=0))
    need = jnp.maximum(need, lax.ppermute(need, "row", [(0, 1), (1, 0), (2, 3), (3, 2)]))
    need = jnp.maximum(need, lax.ppermute(need, "row", [(0, 2), (1, 3), (2, 0), (3, 1)]))
    send_at = send_places(active, counts, offsets, pairs, place, ncol)
    pick_at = pick_places(offsets, pairs, place, own, ncol)

    sums = row_sum(jnp.dot(x_all, both, preferred_element_type=F32), core)
    gate, up = sums[:, :hid], sums[:, hid:]
    sig = jax.nn.sigmoid(gate)
    act = gate * sig
    hidden = (act * up).astype(BF)
    output = scatter_sum(jnp.dot(hidden, wd, preferred_element_type=F32), ncol)
    hidden_grad = row_sum(contract_last(dy_all, wd), core)
    gate_grad = (hidden_grad * up * sig * (1.0 + gate * (1.0 - sig))).astype(BF)
    up_grad = (hidden_grad * act).astype(BF)
    factor = float(x_all.shape[0]) ** (-0.5)
    main, extra = pack_grads(send_at, x_all, gate_grad, up_grad, hidden, dy_all, factor, brows, bcols, ncol)
    got = lax.all_to_all(main, "col", 0, 0, tiled=True)
    input_grad = scatter_sum(contract_last(jnp.concatenate([gate_grad, up_grad], axis=1), both), ncol)

    def with_extra():
        more = lax.all_to_all(extra, "col", 0, 0, tiled=True)
        return pick_blocks(pick_at, jnp.concatenate([got, more], axis=0))

    def without():
        return pick_blocks(pick_at, got)

    grad_blocks = lax.cond(need > MAIN, with_extra, without)
    return (output, input_grad, grad_blocks.reshape(3, 1, 1, own, BLOCK, BLOCK))


def solution(mesh):
    return jax.shard_map(
        shards,
        mesh=mesh,
        in_specs=(
            P("col", "row"),
            P("col", "row"),
            P("row", "col"),
            P("row", "col"),
            P("col", "row"),
            P(None, "row", "col"),
            P(None, "row", "col"),
        ),
        out_specs=(P("col", "row"), P("col", "row"), P(None, "row", "col", None, None, None)),
        check_vma=False,
    )
```

```python
import functools

import jax
import jax.numpy as jnp
from jax import lax
from jax.experimental import pallas as pl
from jax.experimental.pallas import tpu as pltpu
from jax.sharding import PartitionSpec as P

BLOCK = 128
MAIN = 7
EXTRA = 2
LANES = 128
BF = jnp.bfloat16
F32 = jnp.float32


def contract_last(left, right):
    return lax.dot_general(left, right, (((1,), (1,)), ((), ())), preferred_element_type=F32)


def together(go, step, *args):
    shapes = jax.eval_shape(step, *args)
    return lax.cond(go, step, lambda *_: jax.tree.map(lambda v: jnp.zeros(v.shape, v.dtype), shapes), *args)


def plane_groups(ncol):
    return [list(range(ncol // 2)), list(range(ncol // 2, ncol))]


def across(value, ncol):
    return lax.ppermute(value, "col", [(i, (i + ncol // 2) % ncol) for i in range(ncol)])


def gather_rows(part, ncol):
    many = ncol // 2
    copies = jnp.broadcast_to(part[None], (many,) + part.shape).reshape(many * part.shape[0], part.shape[1])
    return plane_exchange(copies, ncol)


def plane_exchange(value, ncol):
    return lax.all_to_all(value, "col", 0, 0, axis_index_groups=plane_groups(ncol), tiled=True)


def add_parts(got, ncol):
    many = ncol // 2
    total = jnp.sum(got.reshape(many, got.shape[0] // many, -1).astype(F32), axis=0)
    rows = total.shape[0] // 2
    return (total[:rows] + across(total[rows:], ncol)).astype(BF)


def tie(*values):
    return lax.optimization_barrier(values)


def row_sum(keep, send):
    pair = [(0, 1), (1, 0), (2, 3), (3, 2)]
    far = [(0, 2), (1, 3), (2, 0), (3, 1)]
    mine = keep + lax.ppermute(send, "row", pair)
    mine = mine + lax.ppermute(mine.astype(BF), "row", far).astype(F32)
    return mine, lax.ppermute(mine, "row", pair)


def mask_kernel(bcols, kept_ref, gate_ref, up_ref, down_ref, both_ref, out_ref):
    i = pl.program_id(0)
    count = pl.num_programs(0) * bcols
    for f in range(bcols):
        cut = slice(f * BLOCK, (f + 1) * BLOCK)
        for which, from_ref in ((0, gate_ref), (1, up_ref)):
            keep = kept_ref[which * count + i * bcols + f] > 0
            value = from_ref[:, cut]
            both_ref[:, (which * bcols + f) * BLOCK:(which * bcols + f + 1) * BLOCK] = jnp.where(keep, value, jnp.zeros_like(value))
        keep = kept_ref[2 * count + i * bcols + f] > 0
        value = down_ref[cut, :]
        out_ref[cut, :] = jnp.where(keep, value, jnp.zeros_like(value))


def mask_weights(kept, gate, up, down):
    feat, hid = gate.shape
    bcols = hid // BLOCK
    side = pl.BlockSpec((BLOCK, hid), lambda i: (i, 0))
    flat = pl.BlockSpec((hid, BLOCK), lambda i: (0, i))
    return pl.pallas_call(
        functools.partial(mask_kernel, bcols),
        grid=(feat // BLOCK,),
        out_shape=(jax.ShapeDtypeStruct((feat, 2 * hid), BF), jax.ShapeDtypeStruct((hid, feat), BF)),
        in_specs=[pl.BlockSpec(memory_space=pltpu.SMEM), side, side, flat],
        out_specs=(pl.BlockSpec((BLOCK, 2 * hid), lambda i: (i, 0)), flat),
        compiler_params=pltpu.CompilerParams(vmem_limit_bytes=16 * 2**20),
    )(kept.reshape(-1), gate, up, down)


def put_halves(first, keep_ref, send_ref, lanes, value):
    half = keep_ref.shape[0]

    @pl.when(first)
    def _():
        keep_ref[:, lanes] = value[:half]
        send_ref[:, lanes] = value[half:]

    @pl.when(jnp.logical_not(first))
    def _():
        keep_ref[:, lanes] = value[half:]
        send_ref[:, lanes] = value[:half]


def shares_kernel(feat, cut, down, core_ref, rows_ref, weight_ref, keep_ref, send_ref):
    first = core_ref[0] == 0

    def step(i, carry):
        at = pl.multiple_of(i * cut, cut)
        lanes = pl.ds(at, cut)
        if down:
            value = contract_last(rows_ref[:, :feat], weight_ref[lanes, :])
        else:
            value = jnp.dot(rows_ref[:, :feat], weight_ref[:, lanes], preferred_element_type=F32)
        put_halves(first, keep_ref, send_ref, lanes, value)
        return carry

    lax.fori_loop(0, keep_ref.shape[1] // cut, step, 0)


def shares(core, rows, weight, down):
    feat, wide = weight.shape[::-1] if down else weight.shape
    vmem = pl.BlockSpec(memory_space=pltpu.VMEM)
    shape = jax.ShapeDtypeStruct((rows.shape[0] // 2, wide), F32)
    return pl.pallas_call(
        functools.partial(shares_kernel, feat, 256, down),
        out_shape=(shape, shape),
        in_specs=[pl.BlockSpec(memory_space=pltpu.SMEM)] + [vmem] * 2,
        out_specs=(vmem, vmem),
        compiler_params=pltpu.CompilerParams(vmem_limit_bytes=40 * 2**20),
    )(core, rows, weight)


def hidden_kernel(core_ref, mine_ref, other_ref, down_ref, hidden_ref, part_ref):
    half, hid = mine_ref.shape[0], hidden_ref.shape[1]
    cut = 512

    def point(sums_ref, at):
        gate, up = sums_ref[:, :hid], sums_ref[:, hid:]
        hidden_ref[pl.ds(at, half), :] = (gate * jax.nn.sigmoid(gate) * up).astype(BF)

    place = pl.multiple_of(core_ref[0] * half, half)
    point(mine_ref, place)
    point(other_ref, pl.multiple_of(half - place, half))

    def step(i, carry):
        lanes = pl.ds(pl.multiple_of(i * cut, cut), cut)
        part_ref[:, lanes] = jnp.dot(hidden_ref[...], down_ref[:, lanes], preferred_element_type=F32).astype(BF)
        return carry

    lax.fori_loop(0, part_ref.shape[1] // cut, step, 0)


def hidden_stage(core, mine, other, wd):
    hid, feat = wd.shape
    rows = 2 * mine.shape[0]
    vmem = pl.BlockSpec(memory_space=pltpu.VMEM)
    return pl.pallas_call(
        hidden_kernel,
        out_shape=(jax.ShapeDtypeStruct((rows, hid), BF), jax.ShapeDtypeStruct((rows, feat), BF)),
        in_specs=[pl.BlockSpec(memory_space=pltpu.SMEM)] + [vmem] * 3,
        out_specs=(vmem, vmem),
        compiler_params=pltpu.CompilerParams(vmem_limit_bytes=40 * 2**20),
    )(core, mine, other, wd)


def grads_kernel(core_ref, mine_ref, other_ref, back_ref, back_other_ref, both_ref, grads_ref, part_ref):
    half, hid = back_ref.shape
    cut = 512

    def point(sums_ref, hidden_grad_ref, at):
        gate, up, hidden_grad = sums_ref[:, :hid], sums_ref[:, hid:], hidden_grad_ref[...]
        sig = jax.nn.sigmoid(gate)
        rows = pl.ds(at, half)
        grads_ref[rows, :hid] = (hidden_grad * up * sig * (1.0 + gate * (1.0 - sig))).astype(BF)
        grads_ref[rows, hid:] = (hidden_grad * (gate * sig)).astype(BF)

    place = pl.multiple_of(core_ref[0] * half, half)
    point(mine_ref, back_ref, place)
    point(other_ref, back_other_ref, pl.multiple_of(half - place, half))

    def step(i, carry):
        lanes = pl.ds(pl.multiple_of(i * cut, cut), cut)
        part_ref[:, lanes] = contract_last(grads_ref[...], both_ref[lanes, :]).astype(BF)
        return carry

    lax.fori_loop(0, part_ref.shape[1] // cut, step, 0)


def grads_stage(core, sums, back, both):
    feat, wide = both.shape
    rows = 2 * back[0].shape[0]
    vmem = pl.BlockSpec(memory_space=pltpu.VMEM)
    return pl.pallas_call(
        grads_kernel,
        out_shape=(jax.ShapeDtypeStruct((rows, wide), BF), jax.ShapeDtypeStruct((rows, feat), BF)),
        in_specs=[pl.BlockSpec(memory_space=pltpu.SMEM)] + [vmem] * 5,
        out_specs=(vmem, vmem),
        compiler_params=pltpu.CompilerParams(vmem_limit_bytes=44 * 2**20),
    )(core, *sums, *back, both)


def dot_rows(left, right):
    return lax.dot_general(left, right, (((0,), (0,)), ((), ())), preferred_element_type=F32)


def pack_kernel(factor, brows, bcols, group, where_ref, x_ref, dy_ref, grads_ref, hidden_ref, main_ref, extra_ref):
    cut = main_ref.shape[0]
    wide = group * BLOCK
    hid = bcols * BLOCK

    def store(which, d, f, block):
        at = where_ref[which * brows * bcols + d * bcols + f]

        @pl.when((at >= 0) & (at < cut))
        def _():
            main_ref[at] = block

        @pl.when(at >= cut)
        def _():
            extra_ref[at - cut] = block

    def step(i, carry):
        lanes = pl.ds(pl.multiple_of(i * wide, wide), wide)
        x = x_ref[:, lanes]
        for which in (0, 1):
            tile = (dot_rows(x, grads_ref[:, which * hid:(which + 1) * hid]) * factor).astype(BF)
            for u in range(group):
                for f in range(bcols):
                    store(which, i * group + u, f, tile[u * BLOCK:(u + 1) * BLOCK, f * BLOCK:(f + 1) * BLOCK])
        tile = (dot_rows(hidden_ref[...], dy_ref[:, lanes]) * factor).astype(BF)
        for u in range(group):
            for f in range(bcols):
                store(2, i * group + u, f, tile[f * BLOCK:(f + 1) * BLOCK, u * BLOCK:(u + 1) * BLOCK])
        return carry

    lax.fori_loop(0, brows // group, step, 0)


def pack_grads(where, x_all, dy_all, grads, hidden, factor, brows, bcols, ncol):
    vmem = pl.BlockSpec(memory_space=pltpu.VMEM)
    return pl.pallas_call(
        functools.partial(pack_kernel, factor, brows, bcols, 4),
        out_shape=(
            jax.ShapeDtypeStruct((ncol * MAIN, BLOCK, BLOCK), BF),
            jax.ShapeDtypeStruct((ncol * EXTRA, BLOCK, BLOCK), BF),
        ),
        in_specs=[pl.BlockSpec(memory_space=pltpu.SMEM)] + [vmem] * 4,
        out_specs=(vmem, vmem),
        compiler_params=pltpu.CompilerParams(vmem_limit_bytes=48 * 2**20),
    )(where, x_all, dy_all, grads, hidden)


def pick_kernel(count, from_ref, got_ref, out_ref):
    def step(i, carry):
        out_ref[i] = got_ref[from_ref[i]]
        return carry

    lax.fori_loop(0, count, step, 0, unroll=4)


def pick_blocks(source, got):
    vmem = pl.BlockSpec(memory_space=pltpu.VMEM)
    count = source.shape[0]
    return pl.pallas_call(
        functools.partial(pick_kernel, count),
        out_shape=jax.ShapeDtypeStruct((count, BLOCK, BLOCK), BF),
        in_specs=[pl.BlockSpec(memory_space=pltpu.SMEM), vmem],
        out_specs=vmem,
        compiler_params=pltpu.CompilerParams(vmem_limit_bytes=32 * 2**20),
    )(source, got)


def pair_counts(counts, offsets, ncol):
    owners = jnp.arange(ncol, dtype=jnp.int32)
    first = (owners[None, None, :] - offsets[:, :, None]) % ncol
    return (counts[:, :, None] - first + ncol - 1) // ncol


def send_places(active, counts, offsets, pairs, place, ncol):
    flat = active.reshape(3, -1)
    local = jnp.cumsum(flat, axis=1) - 1
    mine = offsets[:, place][:, None]
    owner = (mine + local) % ncol
    ahead = jnp.cumsum(pairs, axis=0) - pairs
    ahead = ahead[:, place]
    before = jnp.sum(jnp.where(owner[:, :, None] == jnp.arange(ncol)[None, None, :], ahead[:, None, :], 0), axis=2)
    slot = before + local // ncol
    at = jnp.where(slot < MAIN, owner * MAIN + slot, ncol * MAIN + owner * EXTRA + slot - MAIN)
    return jnp.where(flat > 0, at, -1).reshape(-1).astype(jnp.int32)


def pick_places(offsets, pairs, place, own, ncol):
    wanted = jnp.arange(own, dtype=jnp.int32)[None, :] * ncol + place
    source = jnp.sum((offsets[:, None, :] <= wanted[:, :, None]).astype(jnp.int32), axis=2) - 1
    ahead = (jnp.cumsum(pairs, axis=0) - pairs)[:, :, place]
    here = source[:, :, None] == jnp.arange(ncol)[None, None, :]
    start = jnp.sum(jnp.where(here, offsets[:, None, :], 0), axis=2)
    before = jnp.sum(jnp.where(here, ahead[:, None, :], 0), axis=2)
    slot = before + (wanted - start) // ncol
    at = jnp.where(slot < MAIN, source * MAIN + slot, ncol * MAIN + source * EXTRA + slot - MAIN)
    return at.reshape(-1).astype(jnp.int32)


def shards(tokens, cotangent, gate_weight, up_weight, down_weight, kept, regrown):
    feat, hid = gate_weight.shape
    brows, bcols = kept.shape[1], kept.shape[2]
    ncol = lax.axis_size("col")
    place = lax.axis_index("col")
    core = (lax.axis_index("row") % 2).astype(jnp.int32).reshape(1)
    own = brows * bcols // 4
    rows = tokens.shape[0]
    active = kept + regrown
    tally = jnp.sum(active, axis=(1, 2))
    note = jnp.zeros((rows, LANES), BF).at[0, :3].set(tally.astype(BF))
    go = jnp.sum(tally) >= 0

    mine = jnp.concatenate([tokens, note, cotangent], axis=1)
    joint = jnp.concatenate([mine, across(mine, ncol)], axis=0)
    x_all = gather_rows(joint[:, :feat + LANES], ncol)
    both, wd = mask_weights(kept, gate_weight, up_weight, down_weight)
    x_all, both, wd, late = tie(x_all, both, wd, joint[:, feat + LANES:])
    dy_all = gather_rows(late, ncol)

    near = x_all.reshape(ncol // 2, 2, rows, -1)[:, :, 0, feat:feat + 3].astype(jnp.int32)
    near = jnp.where(place < ncol // 2, near, near[:, ::-1])
    counts = near.transpose(2, 1, 0).reshape(3, ncol)
    offsets = jnp.cumsum(counts, axis=1) - counts
    pairs = pair_counts(counts, offsets, ncol)
    need = jnp.max(jnp.sum(pairs, axis=0))
    send_at = send_places(active, counts, offsets, pairs, place, ncol)
    pick_at = pick_places(offsets, pairs, place, own, ncol)

    def forward(x_all, both, wd):
        sums = row_sum(*shares(core, x_all, both, False))
        return sums + tuple(hidden_stage(core, *sums, wd))

    def backward(dy_all, sums, need, both, wd):
        back = row_sum(*shares(core, dy_all, wd, True))
        need = jnp.maximum(need, lax.ppermute(need, "row", [(0, 1), (1, 0), (2, 3), (3, 2)]))
        need = jnp.maximum(need, lax.ppermute(need, "row", [(0, 2), (1, 3), (2, 0), (3, 1)]))
        return (need,) + tuple(grads_stage(core, sums, back, both))

    gate_up_mine, gate_up_other, hidden, out_part = together(go, forward, x_all, both, wd)
    dy_all, gate_up_mine, gate_up_other, out_part, send_at, pick_at, need = tie(
        dy_all, gate_up_mine, gate_up_other, out_part, send_at, pick_at, need)
    got_out = plane_exchange(out_part, ncol)
    need, grads, in_part = together(go, backward, dy_all, (gate_up_mine, gate_up_other), need, both, wd)
    got_out, in_part, need = tie(got_out, in_part, need)
    got_in = plane_exchange(in_part, ncol)
    output = add_parts(got_out, ncol)
    factor = float(rows * ncol) ** (-0.5)
    main, extra = pack_grads(send_at, x_all, dy_all, grads, hidden, factor, brows, bcols, ncol)
    got_in, main, extra, output = tie(got_in, main, extra, output)
    got = lax.all_to_all(main, "col", 0, 0, tiled=True)
    input_grad = add_parts(got_in, ncol)

    def with_extra():
        more = lax.all_to_all(extra, "col", 0, 0, tiled=True)
        return pick_blocks(pick_at, jnp.concatenate([got, more], axis=0))

    def without():
        return pick_blocks(pick_at, got)

    grad_blocks = lax.cond(need > MAIN, with_extra, without)
    return (output, input_grad, grad_blocks.reshape(3, 1, 1, own, BLOCK, BLOCK))


def solution(mesh):
    return jax.shard_map(
        shards,
        mesh=mesh,
        in_specs=(
            P("col", "row"),
            P("col", "row"),
            P("row", "col"),
            P("row", "col"),
            P("col", "row"),
            P(None, "row", "col"),
            P(None, "row", "col"),
        ),
        out_specs=(P("col", "row"), P("col", "row"), P(None, "row", "col", None, None, None)),
        check_vma=False,
    )
```

```python
import functools

import jax
import jax.numpy as jnp
from jax import lax
from jax.experimental import pallas as pl
from jax.experimental.pallas import tpu as pltpu
from jax.sharding import PartitionSpec as P

BLOCK = 128
MAIN = 7
EXTRA = 2
LANES = 128
BF = jnp.bfloat16
F32 = jnp.float32


def contract_last(left, right):
    return lax.dot_general(left, right, (((1,), (1,)), ((), ())), preferred_element_type=F32)


def together(go, step, *args):
    shapes = jax.eval_shape(step, *args)
    return lax.cond(go, step, lambda *_: jax.tree.map(lambda v: jnp.zeros(v.shape, v.dtype), shapes), *args)


def plane_groups(ncol):
    return [list(range(ncol // 2)), list(range(ncol // 2, ncol))]


def across(value, ncol):
    return lax.ppermute(value, "col", [(i, (i + ncol // 2) % ncol) for i in range(ncol)])


def copies(part, many):
    return jnp.broadcast_to(part[None], (many,) + part.shape).reshape(many * part.shape[0], part.shape[1])


def plane_exchange(value, ncol):
    return lax.all_to_all(value, "col", 0, 0, axis_index_groups=plane_groups(ncol), tiled=True)


def add_parts(got, ncol):
    many = ncol // 2
    total = jnp.sum(got.reshape(many, got.shape[0] // many, -1).astype(F32), axis=0)
    rows = total.shape[0] // 2
    return (total[:rows] + across(total[rows:], ncol)).astype(BF)


def tie(*values):
    return lax.optimization_barrier(values)


def row_sum(keep, send):
    pair = [(0, 1), (1, 0), (2, 3), (3, 2)]
    far = [(0, 2), (1, 3), (2, 0), (3, 1)]
    mine = keep + lax.ppermute(send, "row", pair)
    mine = mine + lax.ppermute(mine.astype(BF), "row", far).astype(F32)
    return mine, lax.ppermute(mine, "row", pair)


def mask_kernel(bcols, kept_ref, gate_ref, up_ref, down_ref, both_ref, out_ref):
    i = pl.program_id(0)
    count = pl.num_programs(0) * bcols
    for f in range(bcols):
        cut = slice(f * BLOCK, (f + 1) * BLOCK)
        for which, from_ref in ((0, gate_ref), (1, up_ref)):
            keep = kept_ref[which * count + i * bcols + f] > 0
            value = from_ref[:, cut]
            both_ref[:, (which * bcols + f) * BLOCK:(which * bcols + f + 1) * BLOCK] = jnp.where(keep, value, jnp.zeros_like(value))
        keep = kept_ref[2 * count + i * bcols + f] > 0
        value = down_ref[cut, :]
        out_ref[cut, :] = jnp.where(keep, value, jnp.zeros_like(value))


def mask_weights(kept, gate, up, down):
    feat, hid = gate.shape
    bcols = hid // BLOCK
    side = pl.BlockSpec((BLOCK, hid), lambda i: (i, 0))
    flat = pl.BlockSpec((hid, BLOCK), lambda i: (0, i))
    return pl.pallas_call(
        functools.partial(mask_kernel, bcols),
        grid=(feat // BLOCK,),
        out_shape=(jax.ShapeDtypeStruct((feat, 2 * hid), BF), jax.ShapeDtypeStruct((hid, feat), BF)),
        in_specs=[pl.BlockSpec(memory_space=pltpu.SMEM), side, side, flat],
        out_specs=(pl.BlockSpec((BLOCK, 2 * hid), lambda i: (i, 0)), flat),
        compiler_params=pltpu.CompilerParams(vmem_limit_bytes=16 * 2**20),
    )(kept.reshape(-1), gate, up, down)


def shares_kernel(reorder, core_ref, rows_ref, weight_ref, *out_refs):
    keep_ref, send_ref = out_refs[:2]
    half, feat = keep_ref.shape[0], out_refs[2].shape[1] if reorder else rows_ref.shape[1]
    if reorder:
        rows = rows_ref.shape[2]

        @pl.when(pl.program_id(0) == 0)
        def _():
            for chip in range(rows_ref.shape[1]):
                for other in range(2):
                    plane = core_ref[1] if other == 0 else 1 - core_ref[1]
                    at = (2 * chip + other) * rows
                    out_refs[2][at:at + rows, :] = rows_ref[plane, chip, :, :feat]

        value = jnp.dot(out_refs[2][...], weight_ref[...], preferred_element_type=F32)
    else:
        value = contract_last(rows_ref[...], weight_ref[...])

    @pl.when(core_ref[0] == 0)
    def _():
        keep_ref[...] = value[:half]
        send_ref[...] = value[half:]

    @pl.when(core_ref[0] != 0)
    def _():
        keep_ref[...] = value[half:]
        send_ref[...] = value[:half]


def shares(core, rows, weight, reorder):
    vmem = pl.BlockSpec(memory_space=pltpu.VMEM)
    cut = 256
    if reorder:
        (feat, wide), tokens = weight.shape, rows.shape[0] * rows.shape[1] * rows.shape[2]
        part = pl.BlockSpec((feat, cut), lambda i: (0, i))
    else:
        (wide, feat), tokens = weight.shape, rows.shape[0]
        part = pl.BlockSpec((cut, feat), lambda i: (i, 0))
    shape = jax.ShapeDtypeStruct((tokens // 2, wide), F32)
    out = pl.BlockSpec((tokens // 2, cut), lambda i: (0, i))
    more = reorder * (jax.ShapeDtypeStruct((tokens, feat), BF),)
    return pl.pallas_call(
        functools.partial(shares_kernel, reorder),
        grid=(wide // cut,),
        out_shape=(shape, shape) + more,
        in_specs=[pl.BlockSpec(memory_space=pltpu.SMEM), vmem, part],
        out_specs=(out, out) + reorder * (pl.BlockSpec((tokens, feat), lambda i: (0, 0)),),
        compiler_params=pltpu.CompilerParams(vmem_limit_bytes=40 * 2**20),
    )(core, rows, weight)


def hidden_kernel(core_ref, mine_ref, other_ref, down_ref, hidden_ref, part_ref):
    half, hid = mine_ref.shape[0], hidden_ref.shape[1]

    def point(sums_ref, at):
        gate, up = sums_ref[:, :hid], sums_ref[:, hid:]
        hidden_ref[pl.ds(at, half), :] = (gate * jax.nn.sigmoid(gate) * up).astype(BF)

    @pl.when(pl.program_id(0) == 0)
    def _():
        place = pl.multiple_of(core_ref[0] * half, half)
        point(mine_ref, place)
        point(other_ref, pl.multiple_of(half - place, half))

    part_ref[...] = jnp.dot(hidden_ref[...], down_ref[...], preferred_element_type=F32).astype(BF)


def hidden_stage(core, mine, other, wd):
    hid, feat = wd.shape
    cut = 512
    rows = 2 * mine.shape[0]
    vmem = pl.BlockSpec(memory_space=pltpu.VMEM)
    return pl.pallas_call(
        hidden_kernel,
        grid=(feat // cut,),
        out_shape=(jax.ShapeDtypeStruct((rows, hid), BF), jax.ShapeDtypeStruct((rows, feat), BF)),
        in_specs=[pl.BlockSpec(memory_space=pltpu.SMEM), vmem, vmem, pl.BlockSpec((hid, cut), lambda i: (0, i))],
        out_specs=(pl.BlockSpec((rows, hid), lambda i: (0, 0)), pl.BlockSpec((rows, cut), lambda i: (0, i))),
        compiler_params=pltpu.CompilerParams(vmem_limit_bytes=40 * 2**20),
    )(core, mine, other, wd)


def grads_kernel(core_ref, mine_ref, other_ref, back_ref, back_other_ref, both_ref, grads_ref, part_ref):
    half, hid = back_ref.shape

    def point(sums_ref, hidden_grad_ref, at):
        gate, up, hidden_grad = sums_ref[:, :hid], sums_ref[:, hid:], hidden_grad_ref[...]
        sig = jax.nn.sigmoid(gate)
        rows = pl.ds(at, half)
        grads_ref[rows, :hid] = (hidden_grad * up * sig * (1.0 + gate * (1.0 - sig))).astype(BF)
        grads_ref[rows, hid:] = (hidden_grad * (gate * sig)).astype(BF)

    @pl.when(pl.program_id(0) == 0)
    def _():
        place = pl.multiple_of(core_ref[0] * half, half)
        point(mine_ref, back_ref, place)
        point(other_ref, back_other_ref, pl.multiple_of(half - place, half))

    part_ref[...] = contract_last(grads_ref[...], both_ref[...]).astype(BF)


def grads_stage(core, sums, back, both):
    feat, wide = both.shape
    cut = 512
    rows = 2 * back[0].shape[0]
    vmem = pl.BlockSpec(memory_space=pltpu.VMEM)
    return pl.pallas_call(
        grads_kernel,
        grid=(feat // cut,),
        out_shape=(jax.ShapeDtypeStruct((rows, wide), BF), jax.ShapeDtypeStruct((rows, feat), BF)),
        in_specs=[pl.BlockSpec(memory_space=pltpu.SMEM)] + [vmem] * 4 + [pl.BlockSpec((cut, wide), lambda i: (i, 0))],
        out_specs=(pl.BlockSpec((rows, wide), lambda i: (0, 0)), pl.BlockSpec((rows, cut), lambda i: (0, i))),
        compiler_params=pltpu.CompilerParams(vmem_limit_bytes=44 * 2**20),
    )(core, *sums, *back, both)


def dot_rows(left, right):
    return lax.dot_general(left, right, (((0,), (0,)), ((), ())), preferred_element_type=F32)


def pack_kernel(factor, brows, bcols, group, where_ref, x_ref, dy_ref, grads_ref, hidden_ref, main_ref, extra_ref, turned_ref, slots_ref, sems):
    cut = main_ref.shape[0]
    more = extra_ref.shape[0]
    wide = group * BLOCK

    def store(which, d, f, block):
        slots_ref[where_ref[which * brows * bcols + d * bcols + f]] = block

    turned_ref[...] = hidden_ref[...].T

    def step(i, carry):
        lanes = pl.ds(pl.multiple_of(i * wide, wide), wide)
        tile = (dot_rows(x_ref[:, lanes], grads_ref[...]) * factor).astype(BF)
        for which in (0, 1):
            for u in range(group):
                for f in range(bcols):
                    at = (which * bcols + f) * BLOCK
                    store(which, i * group + u, f, tile[u * BLOCK:(u + 1) * BLOCK, at:at + BLOCK])
        tile = (jnp.dot(turned_ref[...], dy_ref[:, lanes], preferred_element_type=F32) * factor).astype(BF)
        for u in range(group):
            for f in range(bcols):
                store(2, i * group + u, f, tile[f * BLOCK:(f + 1) * BLOCK, u * BLOCK:(u + 1) * BLOCK])
        return carry

    lax.fori_loop(0, brows // group, step, 0)
    first = pltpu.make_async_copy(slots_ref.at[pl.ds(0, cut)], main_ref, sems.at[0])
    second = pltpu.make_async_copy(slots_ref.at[pl.ds(cut, more)], extra_ref, sems.at[1])
    first.start()
    second.start()
    first.wait()
    second.wait()


def pack_grads(where, x_all, dy_all, grads, hidden, factor, brows, bcols, ncol):
    vmem = pl.BlockSpec(memory_space=pltpu.VMEM)
    return pl.pallas_call(
        functools.partial(pack_kernel, factor, brows, bcols, 4),
        out_shape=(
            jax.ShapeDtypeStruct((ncol * MAIN, BLOCK, BLOCK), BF),
            jax.ShapeDtypeStruct((ncol * EXTRA, BLOCK, BLOCK), BF),
        ),
        in_specs=[pl.BlockSpec(memory_space=pltpu.SMEM)] + [vmem] * 4,
        out_specs=(pl.BlockSpec(memory_space=pl.ANY),) * 2,
        scratch_shapes=[
            pltpu.VMEM((hidden.shape[1], hidden.shape[0]), BF),
            pltpu.VMEM((ncol * (MAIN + EXTRA) + 1, BLOCK, BLOCK), BF),
            pltpu.SemaphoreType.DMA((2,)),
        ],
        compiler_params=pltpu.CompilerParams(vmem_limit_bytes=48 * 2**20),
    )(where, x_all, dy_all, grads, hidden)


def pick_kernel(count, from_ref, got_ref, out_ref, sem):
    def start(i, carry):
        pltpu.make_async_copy(got_ref.at[from_ref[i]], out_ref.at[i], sem).start()
        return carry

    lax.fori_loop(0, count, start, 0, unroll=4)
    pltpu.make_async_copy(got_ref.at[pl.ds(0, count)], out_ref, sem).wait()


def pick_blocks(source, got):
    count = source.shape[0]
    return pl.pallas_call(
        functools.partial(pick_kernel, count),
        out_shape=jax.ShapeDtypeStruct((count, BLOCK, BLOCK), BF),
        in_specs=[pl.BlockSpec(memory_space=pltpu.SMEM), pl.BlockSpec(memory_space=pl.ANY)],
        out_specs=pl.BlockSpec(memory_space=pl.ANY),
        scratch_shapes=[pltpu.SemaphoreType.DMA],
    )(source, got)


def pair_counts(counts, offsets, ncol):
    owners = jnp.arange(ncol, dtype=jnp.int32)
    first = (owners[None, None, :] - offsets[:, :, None]) % ncol
    return (counts[:, :, None] - first + ncol - 1) // ncol


def send_places(active, counts, offsets, pairs, place, ncol):
    flat = active.reshape(3, -1)
    local = jnp.cumsum(flat, axis=1) - 1
    mine = offsets[:, place][:, None]
    owner = (mine + local) % ncol
    ahead = jnp.cumsum(pairs, axis=0) - pairs
    ahead = ahead[:, place]
    before = jnp.sum(jnp.where(owner[:, :, None] == jnp.arange(ncol)[None, None, :], ahead[:, None, :], 0), axis=2)
    slot = before + local // ncol
    at = jnp.where(slot < MAIN, owner * MAIN + slot, ncol * MAIN + owner * EXTRA + slot - MAIN)
    return jnp.where(flat > 0, at, ncol * (MAIN + EXTRA)).reshape(-1).astype(jnp.int32)


def pick_places(offsets, pairs, place, own, ncol):
    wanted = jnp.arange(own, dtype=jnp.int32)[None, :] * ncol + place
    source = jnp.sum((offsets[:, None, :] <= wanted[:, :, None]).astype(jnp.int32), axis=2) - 1
    ahead = (jnp.cumsum(pairs, axis=0) - pairs)[:, :, place]
    here = source[:, :, None] == jnp.arange(ncol)[None, None, :]
    start = jnp.sum(jnp.where(here, offsets[:, None, :], 0), axis=2)
    before = jnp.sum(jnp.where(here, ahead[:, None, :], 0), axis=2)
    slot = before + (wanted - start) // ncol
    at = jnp.where(slot < MAIN, source * MAIN + slot, ncol * MAIN + source * EXTRA + slot - MAIN)
    return at.reshape(-1).astype(jnp.int32)


def shards(tokens, cotangent, gate_weight, up_weight, down_weight, kept, regrown):
    feat, hid = gate_weight.shape
    brows, bcols = kept.shape[1], kept.shape[2]
    ncol = lax.axis_size("col")
    place = lax.axis_index("col")
    core = jnp.stack([lax.axis_index("row") % 2, place // (ncol // 2)]).astype(jnp.int32)
    own = brows * bcols // 4
    rows = tokens.shape[0]
    active = kept + regrown
    tally = jnp.sum(active, axis=(1, 2))
    note = jnp.zeros((rows, LANES), BF).at[0, :3].set(tally.astype(BF))
    go = jnp.sum(tally) >= 0

    x_all = lax.all_to_all(copies(jnp.concatenate([tokens, note], axis=1), ncol), "col", 0, 0, tiled=True)
    both, wd = mask_weights(kept, gate_weight, up_weight, down_weight)
    joint = jnp.concatenate([cotangent, across(cotangent, ncol)], axis=0)
    x_all, both, wd, late = tie(x_all, both, wd, copies(joint, ncol // 2))
    dy_all = plane_exchange(late, ncol)

    def forward(x_all, both, wd):
        keep, send, x_all = shares(core, x_all.reshape(2, ncol // 2, rows, -1), both, True)
        sums = row_sum(keep, send)
        return sums, hidden_stage(core, *sums, wd), x_all

    def backward(note, dy_all, sums, both, wd):
        counts = note.astype(jnp.int32).T
        offsets = jnp.cumsum(counts, axis=1) - counts
        pairs = pair_counts(counts, offsets, ncol)
        need = jnp.max(jnp.sum(pairs, axis=0))
        send_at = send_places(active, counts, offsets, pairs, place, ncol)
        pick_at = pick_places(offsets, pairs, place, own, ncol)
        back = row_sum(*shares(core, dy_all, wd, False))
        return grads_stage(core, sums, back, both), (send_at, pick_at, need)

    def blocks(send_at, need, x_all, dy_all, grads, hidden):
        need = jnp.maximum(need, lax.ppermute(need, "row", [(0, 1), (1, 0), (2, 3), (3, 2)]))
        need = jnp.maximum(need, lax.ppermute(need, "row", [(0, 2), (1, 3), (2, 0), (3, 1)]))
        factor = float(rows * ncol) ** (-0.5)
        return pack_grads(send_at, x_all, dy_all, grads, hidden, factor, brows, bcols, ncol), need

    note = x_all.reshape(ncol, rows, -1)[:, 0, feat:feat + 3]
    sums, (hidden, out_part), x_all = together(go, forward, x_all, both, wd)
    dy_all, sums, out_part = tie(dy_all, sums, out_part)
    got_out = plane_exchange(out_part, ncol)
    (grads, in_part), (send_at, pick_at, need) = together(go, backward, note, dy_all, sums, both, wd)
    got_out, in_part = tie(got_out, in_part)
    got_in = plane_exchange(in_part, ncol)
    (main, extra), need = together(go, blocks, send_at, need, x_all, dy_all, grads, hidden)
    output = add_parts(got_out, ncol)
    got_in, main, extra, output, need = tie(got_in, main, extra, output, need)
    got = lax.all_to_all(main, "col", 0, 0, tiled=True)
    input_grad = add_parts(got_in, ncol)

    def with_extra():
        more = lax.all_to_all(extra, "col", 0, 0, tiled=True)
        return pick_blocks(pick_at, jnp.concatenate([got, more], axis=0))

    def without():
        return pick_blocks(pick_at, got)

    grad_blocks = lax.cond(need > MAIN, with_extra, without)
    return (output, input_grad, grad_blocks.reshape(3, 1, 1, own, BLOCK, BLOCK))


def solution(mesh):
    return jax.shard_map(
        shards,
        mesh=mesh,
        in_specs=(
            P("col", "row"),
            P("col", "row"),
            P("row", "col"),
            P("row", "col"),
            P("col", "row"),
            P(None, "row", "col"),
            P(None, "row", "col"),
        ),
        out_specs=(P("col", "row"), P("col", "row"), P(None, "row", "col", None, None, None)),
        check_vma=False,
    )
```

```python
import functools

import jax
import jax.numpy as jnp
from jax import lax
from jax.experimental import pallas as pl
from jax.experimental.pallas import tpu as pltpu
from jax.sharding import PartitionSpec as P

BLOCK = 128
MAIN = 6
EXTRA = 3
HAND = 16
LANES = 128
BF = jnp.bfloat16
F32 = jnp.float32


def contract_last(left, right):
    return lax.dot_general(left, right, (((1,), (1,)), ((), ())), preferred_element_type=F32)


def together(go, step, *args):
    shapes = jax.eval_shape(step, *args)
    return lax.cond(go, step, lambda *_: jax.tree.map(lambda v: jnp.zeros(v.shape, v.dtype), shapes), *args)


def plane_groups(ncol):
    return [list(range(ncol // 2)), list(range(ncol // 2, ncol))]


def across(value, ncol):
    return lax.ppermute(value, "col", [(i, (i + ncol // 2) % ncol) for i in range(ncol)])


def copies(part, many):
    return jnp.broadcast_to(part[None], (many,) + part.shape).reshape(many * part.shape[0], part.shape[1])


def plane_exchange(value, ncol):
    return lax.all_to_all(value, "col", 0, 0, axis_index_groups=plane_groups(ncol), tiled=True)


def add_parts(got, ncol):
    many = ncol // 2
    total = jnp.sum(got.reshape(many, got.shape[0] // many, -1).astype(F32), axis=0)
    rows = total.shape[0] // 2
    return (total[:rows] + across(total[rows:], ncol)).astype(BF)


def tie(*values):
    return lax.optimization_barrier(values)


def swap_cores(value):
    return lax.ppermute(value, "row", [(0, 1), (1, 0), (2, 3), (3, 2)])


def swap_far(value):
    return lax.ppermute(value, "row", [(0, 2), (1, 3), (2, 0), (3, 1)])


def row_sum(keep, send):
    mine = keep + swap_cores(send)
    return mine + swap_far(mine.astype(BF)).astype(F32)


def mask_kernel(bcols, kept_ref, gate_ref, up_ref, down_ref, both_ref, out_ref):
    i = pl.program_id(0)
    count = pl.num_programs(0) * bcols
    for f in range(bcols):
        cut = slice(f * BLOCK, (f + 1) * BLOCK)
        for which, from_ref in ((0, gate_ref), (1, up_ref)):
            keep = kept_ref[which * count + i * bcols + f] > 0
            value = from_ref[:, cut]
            both_ref[:, (which * bcols + f) * BLOCK:(which * bcols + f + 1) * BLOCK] = jnp.where(keep, value, jnp.zeros_like(value))
        keep = kept_ref[2 * count + i * bcols + f] > 0
        value = down_ref[cut, :]
        out_ref[cut, :] = jnp.where(keep, value, jnp.zeros_like(value))


def mask_weights(kept, gate, up, down):
    feat, hid = gate.shape
    bcols = hid // BLOCK
    side = pl.BlockSpec((BLOCK, hid), lambda i: (i, 0))
    flat = pl.BlockSpec((hid, BLOCK), lambda i: (0, i))
    return pl.pallas_call(
        functools.partial(mask_kernel, bcols),
        grid=(feat // BLOCK,),
        out_shape=(jax.ShapeDtypeStruct((feat, 2 * hid), BF), jax.ShapeDtypeStruct((hid, feat), BF)),
        in_specs=[pl.BlockSpec(memory_space=pltpu.SMEM), side, side, flat],
        out_specs=(pl.BlockSpec((BLOCK, 2 * hid), lambda i: (i, 0)), flat),
        compiler_params=pltpu.CompilerParams(vmem_limit_bytes=16 * 2**20),
    )(kept.reshape(-1), gate, up, down)


def shares_kernel(reorder, core_ref, rows_ref, weight_ref, *out_refs):
    keep_ref, send_ref = out_refs[:2]
    half, feat = keep_ref.shape[0], out_refs[2].shape[1] if reorder else rows_ref.shape[1]
    if reorder:
        rows = rows_ref.shape[2]

        @pl.when(pl.program_id(0) == 0)
        def _():
            for chip in range(rows_ref.shape[1]):
                for other in range(2):
                    plane = core_ref[1] if other == 0 else 1 - core_ref[1]
                    at = (2 * chip + other) * rows
                    out_refs[2][at:at + rows, :] = rows_ref[plane, chip, :, :feat]

        value = jnp.dot(out_refs[2][...], weight_ref[...], preferred_element_type=F32)
    else:
        value = contract_last(rows_ref[...], weight_ref[...])

    @pl.when(core_ref[0] == 0)
    def _():
        keep_ref[...] = value[:half]
        send_ref[...] = value[half:]

    @pl.when(core_ref[0] != 0)
    def _():
        keep_ref[...] = value[half:]
        send_ref[...] = value[:half]


def shares(core, rows, weight, reorder):
    vmem = pl.BlockSpec(memory_space=pltpu.VMEM)
    cut = 256
    if reorder:
        (feat, wide), tokens = weight.shape, rows.shape[0] * rows.shape[1] * rows.shape[2]
        part = pl.BlockSpec((feat, cut), lambda i: (0, i))
    else:
        (wide, feat), tokens = weight.shape, rows.shape[0]
        part = pl.BlockSpec((cut, feat), lambda i: (i, 0))
    shape = jax.ShapeDtypeStruct((tokens // 2, wide), F32)
    out = pl.BlockSpec((tokens // 2, cut), lambda i: (0, i))
    more = reorder * (jax.ShapeDtypeStruct((tokens, feat), BF),)
    return pl.pallas_call(
        functools.partial(shares_kernel, reorder),
        grid=(wide // cut,),
        out_shape=(shape, shape) + more,
        in_specs=[pl.BlockSpec(memory_space=pltpu.SMEM), vmem, part],
        out_specs=(out, out) + reorder * (pl.BlockSpec((tokens, feat), lambda i: (0, 0)),),
        compiler_params=pltpu.CompilerParams(vmem_limit_bytes=40 * 2**20),
    )(core, rows, weight)


def hidden_kernel(core_ref, mine_ref, other_ref, down_ref, hidden_ref, part_ref):
    half = mine_ref.shape[0]

    @pl.when(pl.program_id(0) == 0)
    def _():
        place = pl.multiple_of(core_ref[0] * half, half)
        hidden_ref[pl.ds(place, half), :] = mine_ref[...]
        hidden_ref[pl.ds(pl.multiple_of(half - place, half), half), :] = other_ref[...]

    part_ref[...] = jnp.dot(hidden_ref[...], down_ref[...], preferred_element_type=F32).astype(BF)


def hidden_stage(core, mine, other, wd):
    hid, feat = wd.shape
    cut = 512
    rows = 2 * mine.shape[0]
    vmem = pl.BlockSpec(memory_space=pltpu.VMEM)
    return pl.pallas_call(
        hidden_kernel,
        grid=(feat // cut,),
        out_shape=(jax.ShapeDtypeStruct((rows, hid), BF), jax.ShapeDtypeStruct((rows, feat), BF)),
        in_specs=[pl.BlockSpec(memory_space=pltpu.SMEM), vmem, vmem, pl.BlockSpec((hid, cut), lambda i: (0, i))],
        out_specs=(pl.BlockSpec((rows, hid), lambda i: (0, 0)), pl.BlockSpec((rows, cut), lambda i: (0, i))),
        compiler_params=pltpu.CompilerParams(vmem_limit_bytes=40 * 2**20),
    )(core, mine, other, wd)


def grads_kernel(core_ref, mine_ref, other_ref, back_ref, back_other_ref, both_ref, grads_ref, part_ref):
    half, hid = back_ref.shape

    def point(sums_ref, hidden_grad_ref, at):
        gate, up, hidden_grad = sums_ref[:, :hid], sums_ref[:, hid:], hidden_grad_ref[...]
        sig = jax.nn.sigmoid(gate)
        rows = pl.ds(at, half)
        grads_ref[rows, :hid] = (hidden_grad * up * sig * (1.0 + gate * (1.0 - sig))).astype(BF)
        grads_ref[rows, hid:] = (hidden_grad * (gate * sig)).astype(BF)

    @pl.when(pl.program_id(0) == 0)
    def _():
        place = pl.multiple_of(core_ref[0] * half, half)
        point(mine_ref, back_ref, place)
        point(other_ref, back_other_ref, pl.multiple_of(half - place, half))

    part_ref[...] = contract_last(grads_ref[...], both_ref[...]).astype(BF)


def grads_stage(core, sums, back, both):
    feat, wide = both.shape
    cut = 512
    rows = 2 * back[0].shape[0]
    vmem = pl.BlockSpec(memory_space=pltpu.VMEM)
    return pl.pallas_call(
        grads_kernel,
        grid=(feat // cut,),
        out_shape=(jax.ShapeDtypeStruct((rows, wide), BF), jax.ShapeDtypeStruct((rows, feat), BF)),
        in_specs=[pl.BlockSpec(memory_space=pltpu.SMEM)] + [vmem] * 4 + [pl.BlockSpec((cut, wide), lambda i: (i, 0))],
        out_specs=(pl.BlockSpec((rows, wide), lambda i: (0, 0)), pl.BlockSpec((rows, cut), lambda i: (0, i))),
        compiler_params=pltpu.CompilerParams(vmem_limit_bytes=44 * 2**20),
    )(core, *sums, *back, both)


def dot_rows(left, right):
    return lax.dot_general(left, right, (((0,), (0,)), ((), ())), preferred_element_type=F32)


def pack_kernel(factor, brows, bcols, group, where_ref, hand_at_ref, x_ref, dy_ref, grads_ref, hidden_ref, main_ref, extra_ref, hand_ref, turned_ref, slots_ref, sems):
    cut = main_ref.shape[0]
    more = extra_ref.shape[0]
    wide = group * BLOCK

    def store(which, d, f, block):
        slots_ref[where_ref[which, d * bcols + f]] = block

    turned_ref[...] = hidden_ref[...].T

    def step(i, carry):
        lanes = pl.ds(pl.multiple_of(i * wide, wide), wide)
        tile = (dot_rows(x_ref[:, lanes], grads_ref[...]) * factor).astype(BF)
        for which in (0, 1):
            for u in range(group):
                for f in range(bcols):
                    at = (which * bcols + f) * BLOCK
                    store(which, i * group + u, f, tile[u * BLOCK:(u + 1) * BLOCK, at:at + BLOCK])
        tile = (jnp.dot(turned_ref[...], dy_ref[:, lanes], preferred_element_type=F32) * factor).astype(BF)
        for u in range(group):
            for f in range(bcols):
                store(2, i * group + u, f, tile[f * BLOCK:(f + 1) * BLOCK, u * BLOCK:(u + 1) * BLOCK])
        return carry

    lax.fori_loop(0, brows // group, step, 0)
    first = pltpu.make_async_copy(slots_ref.at[pl.ds(0, cut)], main_ref, sems.at[0])
    second = pltpu.make_async_copy(slots_ref.at[pl.ds(cut, more)], extra_ref, sems.at[1])
    first.start()
    second.start()
    for t in range(HAND):
        hand_ref[t] = slots_ref[hand_at_ref[0, t]]
    first.wait()
    second.wait()


def pack_grads(where, hand_at, x_all, dy_all, grads, hidden, factor, brows, bcols, ncol):
    vmem = pl.BlockSpec(memory_space=pltpu.VMEM)
    smem = pl.BlockSpec(memory_space=pltpu.SMEM)
    far = pl.BlockSpec(memory_space=pl.ANY)
    return pl.pallas_call(
        functools.partial(pack_kernel, factor, brows, bcols, 4),
        out_shape=tuple(jax.ShapeDtypeStruct((n, BLOCK, BLOCK), BF) for n in (ncol * MAIN, ncol * EXTRA, HAND)),
        in_specs=[smem, smem] + [vmem] * 4,
        out_specs=(far, far, vmem),
        scratch_shapes=[
            pltpu.VMEM((hidden.shape[1], hidden.shape[0]), BF),
            pltpu.VMEM((ncol * (MAIN + EXTRA) + 1, BLOCK, BLOCK), BF),
            pltpu.SemaphoreType.DMA((2,)),
        ],
        compiler_params=pltpu.CompilerParams(vmem_limit_bytes=48 * 2**20),
    )(where, hand_at, x_all, dy_all, grads, hidden)


def insert_kernel(at_ref, got_ref, old_ref, main_ref, spare_ref, sem):
    for t in range(HAND):
        at = at_ref[0, t]

        @pl.when(at >= 0)
        def _():
            pltpu.make_async_copy(got_ref.at[t], main_ref.at[at], sem).start()

        @pl.when(at < 0)
        def _():
            pltpu.make_async_copy(got_ref.at[t], spare_ref.at[t], sem).start()

    pltpu.make_async_copy(got_ref, spare_ref, sem).wait()


def insert_blocks(at, got, main):
    far = pl.BlockSpec(memory_space=pl.ANY)
    return pl.pallas_call(
        insert_kernel,
        out_shape=jax.ShapeDtypeStruct(main.shape, main.dtype),
        in_specs=[pl.BlockSpec(memory_space=pltpu.SMEM), far, far],
        out_specs=far,
        scratch_shapes=[pltpu.VMEM((HAND, BLOCK, BLOCK), BF), pltpu.SemaphoreType.DMA],
        input_output_aliases={2: 0},
    )(at, got, main)


def pick_kernel(own, from_ref, got_ref, out_ref, sem):
    def start(i, carry):
        for m in range(3):
            pltpu.make_async_copy(got_ref.at[from_ref[m, i]], out_ref.at[m * own + i], sem).start()
        return carry

    lax.fori_loop(0, own, start, 0)
    pltpu.make_async_copy(got_ref.at[pl.ds(0, 3 * own)], out_ref, sem).wait()


def pick_blocks(source, got, own):
    return pl.pallas_call(
        functools.partial(pick_kernel, own),
        out_shape=jax.ShapeDtypeStruct((3 * own, BLOCK, BLOCK), BF),
        in_specs=[pl.BlockSpec(memory_space=pltpu.SMEM), pl.BlockSpec(memory_space=pl.ANY)],
        out_specs=pl.BlockSpec(memory_space=pl.ANY),
        scratch_shapes=[pltpu.SemaphoreType.DMA],
    )(source, got)


def index_kernel(ncol, place_ref, notes_ref, local_ref, send_ref, hand_ref, insert_ref, shared_ref, direct_ref, misfit_ref):
    place = place_ref[0]
    half = ncol // 2
    neighbour = (place + half) % ncol
    rows = lax.broadcasted_iota(jnp.int32, (ncol, LANES), 0)
    lanes = lax.broadcasted_iota(jnp.int32, (ncol, LANES), 1)
    inside = lanes < ncol
    zero = jnp.zeros((ncol, LANES), jnp.int32)

    def across_lanes(value):
        return jnp.sum(value.astype(F32), axis=1, keepdims=True).astype(jnp.int32)

    def down_rows(value):
        return jnp.sum(value.astype(F32), axis=0, keepdims=True).astype(jnp.int32)

    def column(matrix, at):
        return across_lanes(jnp.where(lanes == at, matrix, zero))

    def swapped(matrix):
        return jnp.concatenate([matrix[half:], matrix[:half]], axis=0)

    note = notes_ref[...].astype(F32)[:, :, 0, :].reshape(ncol, LANES)
    turned = jnp.concatenate([note] * (LANES // ncol), axis=0).T.astype(jnp.int32)
    total, total_t = zero, zero
    weights = []
    for m in range(3):
        n_row = turned[m:m + 1, :] + zero
        n_col = column(note.astype(jnp.int32), m)
        off_col = across_lanes(jnp.where(lanes < rows, n_row, zero))
        off_row = down_rows(jnp.where(rows < lanes, n_col + zero, zero))
        pairs = jnp.where(inside, (n_col - ((lanes - off_col) & (ncol - 1)) + ncol - 1) // ncol, zero)
        pairs_t = jnp.where(inside, (n_row - ((rows - off_row) & (ncol - 1)) + ncol - 1) // ncol, zero)
        weights.append((off_col, total, column(total_t, place)))
        total, total_t = total + pairs, total_t + pairs_t
    over_t = jnp.maximum(total_t - MAIN, 0)
    over = jnp.maximum(total - MAIN, 0)
    most = jnp.max((total + swapped(total)).astype(F32)) > 2 * MAIN
    many = jnp.max(across_lanes(over).astype(F32)) > HAND
    misfit_ref[0] = (most | many).astype(jnp.int32)

    def ranks(device):
        count = column(over_t, device)
        row = down_rows(jnp.where(rows == device, over, zero))
        rank = lanes - across_lanes(jnp.where(lanes < rows, row + zero, zero))
        return rank, (rank >= 0) & (rank < count)

    rest = ncol * (MAIN + EXTRA)
    rank, hit = ranks(place)
    hand_ref[...] = rest + down_rows(jnp.where(hit, ncol * MAIN + rows * EXTRA + rank - rest, zero))
    rank, hit = ranks(neighbour)
    slot = column(total_t, place) + rank
    insert_ref[...] = down_rows(jnp.where(hit & (slot < MAIN), rows * MAIN + slot + 1, zero)) - 1
    helped = column(swapped(total), place)
    for m, (off_col, ahead, ahead_t) in enumerate(weights):
        start = down_rows(jnp.where(rows == place, off_col + zero, zero))[:, :1]
        local = local_ref[m:m + 1, :]
        owner = (start + local) & (ncol - 1)
        tall = lax.broadcasted_iota(jnp.int32, (ncol, local.shape[1]), 0)
        slot = down_rows(jnp.where(tall == owner, ahead_t, jnp.zeros_like(tall))) + local // ncol
        at = jnp.where(slot < MAIN, owner * MAIN + slot, ncol * MAIN + owner * EXTRA + slot - MAIN)
        send_ref[m:m + 1, :] = jnp.where(local < 0, rest, at)
        wanted = lax.broadcasted_iota(jnp.int32, (1, LANES), 1) * ncol + place
        source = down_rows((off_col <= wanted).astype(jnp.int32)) - 1
        here = rows == source
        start = down_rows(jnp.where(here, off_col, zero))
        slot = down_rows(jnp.where(here, column(ahead, place), zero)) + (wanted - start) // ncol
        used = down_rows(jnp.where(here, helped, zero))
        near = source * MAIN + slot
        helper = (source + half) & (ncol - 1)
        shared_ref[m:m + 1, :] = jnp.where(slot < MAIN, near, helper * MAIN + used + slot - MAIN)
        direct_ref[m:m + 1, :] = jnp.where(slot < MAIN, near, ncol * MAIN + source * EXTRA + slot - MAIN)


def index_tables(place, x_all, local, feat, ncol):
    planes, chips, rows, _ = x_all.shape
    smem = pl.BlockSpec(memory_space=pltpu.SMEM)
    vmem = pl.BlockSpec(memory_space=pltpu.VMEM)
    wide = jax.ShapeDtypeStruct((1, LANES), jnp.int32)
    three = jax.ShapeDtypeStruct((8, LANES), jnp.int32)
    return pl.pallas_call(
        functools.partial(index_kernel, ncol),
        grid=(1,),
        out_shape=(jax.ShapeDtypeStruct(local.shape, jnp.int32), wide, wide, three, three, jax.ShapeDtypeStruct((1,), jnp.int32)),
        in_specs=[smem, pl.BlockSpec((planes, chips, rows, LANES), lambda i: (0, 0, 0, feat // LANES)), vmem],
        out_specs=(vmem,) * 5 + (smem,),
    )(place.astype(jnp.int32).reshape(1), x_all, local)


def shards(tokens, cotangent, gate_weight, up_weight, down_weight, kept, regrown):
    feat, hid = gate_weight.shape
    brows, bcols = kept.shape[1], kept.shape[2]
    ncol = lax.axis_size("col")
    place = lax.axis_index("col")
    core = jnp.stack([lax.axis_index("row") % 2, place // (ncol // 2)]).astype(jnp.int32)
    own = brows * bcols // 4
    rows = tokens.shape[0]
    active = kept + regrown
    tally = jnp.sum(active, axis=(1, 2))
    note = jnp.zeros((rows, LANES), BF).at[0, :3].set(tally.astype(BF))
    go = jnp.sum(tally) >= 0

    x_all = lax.all_to_all(copies(jnp.concatenate([tokens, note], axis=1), ncol), "col", 0, 0, tiled=True)
    both, wd = mask_weights(kept, gate_weight, up_weight, down_weight)
    joint = jnp.concatenate([cotangent, across(cotangent, ncol)], axis=0)
    flat = active.reshape(3, -1)
    local = jnp.where(flat > 0, jnp.cumsum(flat, axis=1) - 1, -1)
    local = jnp.pad(local, ((0, 5), (0, -flat.shape[1] % LANES)), constant_values=-1)
    x_all, both, wd, late, local = tie(x_all, both, wd, copies(joint, ncol // 2), local)
    dy_all = plane_exchange(late, ncol)

    def forward(spread, both, wd):
        keep, send, x_all = shares(core, spread, both, True)
        gate_up = row_sum(keep, send)
        gate, up = gate_up[:, :hid], gate_up[:, hid:]
        hidden = (gate * jax.nn.sigmoid(gate) * up).astype(BF)
        return gate_up, hidden_stage(core, hidden, swap_cores(hidden), wd), x_all

    def backward(spread, local, dy_all, gate_up, both, wd):
        tables = index_tables(place, spread, local, feat, ncol)
        gate_up_other = swap_cores(gate_up)
        back = row_sum(*shares(core, dy_all, wd, False))
        done = grads_stage(core, (gate_up, gate_up_other), (back, swap_cores(back)), both)
        return done, tables

    def blocks(send_at, hand_at, insert_at, misfit, x_all, dy_all, grads, hidden):
        misfit = jnp.maximum(misfit, swap_cores(misfit))
        misfit = jnp.maximum(misfit, swap_far(misfit))[0]
        factor = float(rows * ncol) ** (-0.5)
        main, extra, hand = pack_grads(send_at, hand_at, x_all, dy_all, grads, hidden, factor, brows, bcols, ncol)
        return insert_blocks(insert_at, across(hand, ncol), main), extra, misfit

    spread = x_all.reshape(2, ncol // 2, rows, -1)
    gate_up, (hidden, out_part), x_all = together(go, forward, spread, both, wd)
    dy_all, gate_up, out_part = tie(dy_all, gate_up, out_part)
    got_out = plane_exchange(out_part, ncol)
    (grads, in_part), (send_at, hand_at, insert_at, shared, direct, misfit) = together(
        go, backward, spread, local, dy_all, gate_up, both, wd)
    got_out, in_part = tie(got_out, in_part)
    got_in = plane_exchange(in_part, ncol)
    main, extra, misfit = together(go, blocks, send_at, hand_at, insert_at, misfit, x_all, dy_all, grads, hidden)
    output = add_parts(got_out, ncol)
    got_in, main, extra, output, misfit = tie(got_in, main, extra, output, misfit)
    got = lax.all_to_all(main, "col", 0, 0, tiled=True)
    input_grad = add_parts(got_in, ncol)

    def with_extra():
        more = lax.all_to_all(extra, "col", 0, 0, tiled=True)
        return pick_blocks(direct, jnp.concatenate([got, more], axis=0), own)

    def without():
        return pick_blocks(shared, got, own)

    grad_blocks = lax.cond(misfit > 0, with_extra, without)
    return (output, input_grad, grad_blocks.reshape(3, 1, 1, own, BLOCK, BLOCK))


def solution(mesh):
    return jax.shard_map(
        shards,
        mesh=mesh,
        in_specs=(
            P("col", "row"),
            P("col", "row"),
            P("row", "col"),
            P("row", "col"),
            P("col", "row"),
            P(None, "row", "col"),
            P(None, "row", "col"),
        ),
        out_specs=(P("col", "row"), P("col", "row"), P(None, "row", "col", None, None, None)),
        check_vma=False,
    )
```

```python
import functools

import jax
import jax.numpy as jnp
from jax import lax
from jax.experimental import pallas as pl
from jax.experimental.pallas import tpu as pltpu
from jax.sharding import PartitionSpec as P

BLOCK = 128
MAIN = 6
EXTRA = 3
HAND = 16
LANES = 128
BF = jnp.bfloat16
F32 = jnp.float32


def contract_last(left, right):
    return lax.dot_general(left, right, (((1,), (1,)), ((), ())), preferred_element_type=F32)


def together(go, step, *args):
    shapes = jax.eval_shape(step, *args)
    return lax.cond(go, step, lambda *_: jax.tree.map(lambda v: jnp.zeros(v.shape, v.dtype), shapes), *args)


def plane_groups(ncol):
    return [list(range(ncol // 2)), list(range(ncol // 2, ncol))]


def across(value, ncol):
    return lax.ppermute(value, "col", [(i, (i + ncol // 2) % ncol) for i in range(ncol)])


def copies(part, many):
    return jnp.broadcast_to(part[None], (many,) + part.shape).reshape(many * part.shape[0], part.shape[1])


def plane_exchange(value, ncol):
    return lax.all_to_all(value, "col", 0, 0, axis_index_groups=plane_groups(ncol), tiled=True)


def add_parts(got, ncol):
    many = ncol // 2
    total = jnp.sum(got.reshape(many, got.shape[0] // many, -1).astype(F32), axis=0)
    rows = total.shape[0] // 2
    return (total[:rows] + across(total[rows:], ncol)).astype(BF)


def tie(*values):
    return lax.optimization_barrier(values)


def swap_cores(value):
    return lax.ppermute(value, "row", [(0, 1), (1, 0), (2, 3), (3, 2)])


def swap_far(value):
    return lax.ppermute(value, "row", [(0, 2), (1, 3), (2, 0), (3, 1)])


def row_sum(keep, send):
    mine = keep + swap_cores(send)
    return mine + swap_far(mine.astype(BF)).astype(F32)


def mask_kernel(bcols, kept_ref, gate_ref, up_ref, down_ref, both_ref, out_ref):
    i = pl.program_id(0)
    count = pl.num_programs(0) * bcols
    for f in range(bcols):
        cut = slice(f * BLOCK, (f + 1) * BLOCK)
        for which, from_ref in ((0, gate_ref), (1, up_ref)):
            keep = kept_ref[which * count + i * bcols + f] > 0
            value = from_ref[:, cut]
            both_ref[:, (which * bcols + f) * BLOCK:(which * bcols + f + 1) * BLOCK] = jnp.where(keep, value, jnp.zeros_like(value))
        keep = kept_ref[2 * count + i * bcols + f] > 0
        value = down_ref[cut, :]
        out_ref[cut, :] = jnp.where(keep, value, jnp.zeros_like(value))


def mask_weights(kept, gate, up, down):
    feat, hid = gate.shape
    bcols = hid // BLOCK
    side = pl.BlockSpec((BLOCK, hid), lambda i: (i, 0))
    flat = pl.BlockSpec((hid, BLOCK), lambda i: (0, i))
    return pl.pallas_call(
        functools.partial(mask_kernel, bcols),
        grid=(feat // BLOCK,),
        out_shape=(jax.ShapeDtypeStruct((feat, 2 * hid), BF), jax.ShapeDtypeStruct((hid, feat), BF)),
        in_specs=[pl.BlockSpec(memory_space=pltpu.SMEM), side, side, flat],
        out_specs=(pl.BlockSpec((BLOCK, 2 * hid), lambda i: (i, 0)), flat),
        compiler_params=pltpu.CompilerParams(vmem_limit_bytes=16 * 2**20),
    )(kept.reshape(-1), gate, up, down)


def shares_kernel(reorder, core_ref, rows_ref, weight_ref, keep_ref, send_ref):
    half = keep_ref.shape[0]
    if reorder:
        value = jnp.dot(rows_ref[...], weight_ref[...], preferred_element_type=F32)
    else:
        value = contract_last(rows_ref[:, :weight_ref.shape[1]], weight_ref[...])

    def put(out_ref, which):
        if not reorder:
            out_ref[...] = value[which * half:(which + 1) * half]
            return
        rows = reorder
        chips = 2 * half // rows // 2
        for chip in range(chips // 2):
            for plane in range(2):
                other = jnp.where(core_ref[1] == plane, 0, 1)
                at = pl.multiple_of(2 * chip * rows + other * rows, rows)
                start = (plane * chips + which * chips // 2 + chip) * rows
                out_ref[pl.ds(at, rows), :] = value[start:start + rows]

    @pl.when(core_ref[0] == 0)
    def _():
        put(keep_ref, 0)
        put(send_ref, 1)

    @pl.when(core_ref[0] != 0)
    def _():
        put(keep_ref, 1)
        put(send_ref, 0)


def shares(core, rows, weight, reorder):
    cut = 256
    if reorder:
        feat, wide = weight.shape
        part = pl.BlockSpec((feat, cut), lambda i: (0, i))
    else:
        wide, feat = weight.shape
        part = pl.BlockSpec((cut, feat), lambda i: (i, 0))
    shape = jax.ShapeDtypeStruct((rows.shape[0] // 2, wide), F32)
    out = pl.BlockSpec((rows.shape[0] // 2, cut), lambda i: (0, i))
    return pl.pallas_call(
        functools.partial(shares_kernel, reorder),
        grid=(wide // cut,),
        out_shape=(shape, shape),
        in_specs=[pl.BlockSpec(memory_space=pltpu.SMEM), pl.BlockSpec(memory_space=pltpu.VMEM), part],
        out_specs=(out, out),
        compiler_params=pltpu.CompilerParams(vmem_limit_bytes=40 * 2**20),
    )(core, rows, weight)


def hidden_kernel(core_ref, mine_ref, other_ref, down_ref, hidden_ref, part_ref):
    half = mine_ref.shape[0]

    @pl.when(pl.program_id(0) == 0)
    def _():
        place = pl.multiple_of(core_ref[0] * half, half)
        hidden_ref[pl.ds(place, half), :] = mine_ref[...]
        hidden_ref[pl.ds(pl.multiple_of(half - place, half), half), :] = other_ref[...]

    part_ref[...] = jnp.dot(hidden_ref[...], down_ref[...], preferred_element_type=F32).astype(BF)


def hidden_stage(core, mine, other, wd):
    hid, feat = wd.shape
    cut = 512
    rows = 2 * mine.shape[0]
    vmem = pl.BlockSpec(memory_space=pltpu.VMEM)
    return pl.pallas_call(
        hidden_kernel,
        grid=(feat // cut,),
        out_shape=(jax.ShapeDtypeStruct((rows, hid), BF), jax.ShapeDtypeStruct((rows, feat), BF)),
        in_specs=[pl.BlockSpec(memory_space=pltpu.SMEM), vmem, vmem, pl.BlockSpec((hid, cut), lambda i: (0, i))],
        out_specs=(pl.BlockSpec((rows, hid), lambda i: (0, 0)), pl.BlockSpec((rows, cut), lambda i: (0, i))),
        compiler_params=pltpu.CompilerParams(vmem_limit_bytes=40 * 2**20),
    )(core, mine, other, wd)


def grads_kernel(core_ref, mine_ref, other_ref, back_ref, back_other_ref, both_ref, grads_ref, part_ref):
    half, hid = back_ref.shape

    def point(sums_ref, hidden_grad_ref, at):
        gate, up, hidden_grad = sums_ref[:, :hid], sums_ref[:, hid:], hidden_grad_ref[...]
        sig = jax.nn.sigmoid(gate)
        rows = pl.ds(at, half)
        grads_ref[rows, :hid] = (hidden_grad * up * sig * (1.0 + gate * (1.0 - sig))).astype(BF)
        grads_ref[rows, hid:] = (hidden_grad * (gate * sig)).astype(BF)

    @pl.when(pl.program_id(0) == 0)
    def _():
        place = pl.multiple_of(core_ref[0] * half, half)
        point(mine_ref, back_ref, place)
        point(other_ref, back_other_ref, pl.multiple_of(half - place, half))

    part_ref[...] = contract_last(grads_ref[...], both_ref[...]).astype(BF)


def grads_stage(core, sums, back, both):
    feat, wide = both.shape
    cut = 1024
    rows = 2 * back[0].shape[0]
    vmem = pl.BlockSpec(memory_space=pltpu.VMEM)
    return pl.pallas_call(
        grads_kernel,
        grid=(feat // cut,),
        out_shape=(jax.ShapeDtypeStruct((rows, wide), BF), jax.ShapeDtypeStruct((rows, feat), BF)),
        in_specs=[pl.BlockSpec(memory_space=pltpu.SMEM)] + [vmem] * 4 + [pl.BlockSpec((cut, wide), lambda i: (i, 0))],
        out_specs=(pl.BlockSpec((rows, wide), lambda i: (0, 0)), pl.BlockSpec((rows, cut), lambda i: (0, i))),
        compiler_params=pltpu.CompilerParams(vmem_limit_bytes=44 * 2**20),
    )(core, *sums, *back, both)


def dot_rows(left, right):
    return lax.dot_general(left, right, (((0,), (0,)), ((), ())), preferred_element_type=F32)


def pack_kernel(factor, brows, bcols, group, core_ref, where_ref, hand_at_ref, x_ref, dy_ref, grads_ref, hidden_ref, main_ref, extra_ref, hand_ref, turned_ref, slots_ref, sems):
    cut = main_ref.shape[0]
    more = extra_ref.shape[0]
    wide = group * BLOCK

    def store(which, d, f, block):
        slots_ref[where_ref[which, d * bcols + f]] = block

    turned_ref[...] = hidden_ref[...].T

    def step(i, carry):
        lanes = pl.ds(pl.multiple_of(i * wide, wide), wide)
        planes = (core_ref[1], 1 - core_ref[1])
        x = jnp.concatenate([x_ref[plane, chip, :, lanes] for chip in range(x_ref.shape[1]) for plane in planes], axis=0)
        tile = (dot_rows(x, grads_ref[...]) * factor).astype(BF)
        for which in (0, 1):
            for u in range(group):
                for f in range(bcols):
                    at = (which * bcols + f) * BLOCK
                    store(which, i * group + u, f, tile[u * BLOCK:(u + 1) * BLOCK, at:at + BLOCK])
        tile = (jnp.dot(turned_ref[...], dy_ref[:, lanes], preferred_element_type=F32) * factor).astype(BF)
        for u in range(group):
            for f in range(bcols):
                store(2, i * group + u, f, tile[f * BLOCK:(f + 1) * BLOCK, u * BLOCK:(u + 1) * BLOCK])
        return carry

    lax.fori_loop(0, brows // group, step, 0)
    first = pltpu.make_async_copy(slots_ref.at[pl.ds(0, cut)], main_ref, sems.at[0])
    second = pltpu.make_async_copy(slots_ref.at[pl.ds(cut, more)], extra_ref, sems.at[1])
    first.start()
    second.start()
    for t in range(HAND):
        hand_ref[t] = slots_ref[hand_at_ref[0, t]]
    first.wait()
    second.wait()


def pack_grads(core, where, hand_at, x_all, dy_all, grads, hidden, factor, brows, bcols, ncol):
    vmem = pl.BlockSpec(memory_space=pltpu.VMEM)
    smem = pl.BlockSpec(memory_space=pltpu.SMEM)
    far = pl.BlockSpec(memory_space=pl.ANY)
    return pl.pallas_call(
        functools.partial(pack_kernel, factor, brows, bcols, 4),
        out_shape=tuple(jax.ShapeDtypeStruct((n, BLOCK, BLOCK), BF) for n in (ncol * MAIN, ncol * EXTRA, HAND)),
        in_specs=[smem] * 3 + [vmem] * 4,
        out_specs=(far, far, vmem),
        scratch_shapes=[
            pltpu.VMEM((hidden.shape[1], hidden.shape[0]), BF),
            pltpu.VMEM((ncol * (MAIN + EXTRA) + 1, BLOCK, BLOCK), BF),
            pltpu.SemaphoreType.DMA((2,)),
        ],
        compiler_params=pltpu.CompilerParams(vmem_limit_bytes=48 * 2**20),
    )(core, where, hand_at, x_all, dy_all, grads, hidden)


def insert_kernel(at_ref, got_ref, old_ref, main_ref, spare_ref, sem):
    for t in range(HAND):
        at = at_ref[0, t]

        @pl.when(at >= 0)
        def _():
            pltpu.make_async_copy(got_ref.at[t], main_ref.at[at], sem).start()

        @pl.when(at < 0)
        def _():
            pltpu.make_async_copy(got_ref.at[t], spare_ref.at[t], sem).start()

    pltpu.make_async_copy(got_ref, spare_ref, sem).wait()


def insert_blocks(at, got, main):
    far = pl.BlockSpec(memory_space=pl.ANY)
    return pl.pallas_call(
        insert_kernel,
        out_shape=jax.ShapeDtypeStruct(main.shape, main.dtype),
        in_specs=[pl.BlockSpec(memory_space=pltpu.SMEM), far, far],
        out_specs=far,
        scratch_shapes=[pltpu.VMEM((HAND, BLOCK, BLOCK), BF), pltpu.SemaphoreType.DMA],
        input_output_aliases={2: 0},
    )(at, got, main)


def pick_kernel(own, from_ref, got_ref, out_ref, sem):
    def start(i, carry):
        for m in range(3):
            pltpu.make_async_copy(got_ref.at[from_ref[m, i]], out_ref.at[m * own + i], sem).start()
        return carry

    lax.fori_loop(0, own, start, 0)
    pltpu.make_async_copy(got_ref.at[pl.ds(0, 3 * own)], out_ref, sem).wait()


def pick_blocks(source, got, own):
    return pl.pallas_call(
        functools.partial(pick_kernel, own),
        out_shape=jax.ShapeDtypeStruct((3 * own, BLOCK, BLOCK), BF),
        in_specs=[pl.BlockSpec(memory_space=pltpu.SMEM), pl.BlockSpec(memory_space=pl.ANY)],
        out_specs=pl.BlockSpec(memory_space=pl.ANY),
        scratch_shapes=[pltpu.SemaphoreType.DMA],
    )(source, got)


def index_kernel(ncol, place_ref, notes_ref, local_ref, send_ref, hand_ref, insert_ref, shared_ref, direct_ref, misfit_ref):
    place = place_ref[0]
    half = ncol // 2
    neighbour = (place + half) % ncol
    rows = lax.broadcasted_iota(jnp.int32, (ncol, LANES), 0)
    lanes = lax.broadcasted_iota(jnp.int32, (ncol, LANES), 1)
    inside = lanes < ncol
    zero = jnp.zeros((ncol, LANES), jnp.int32)

    def across_lanes(value):
        return jnp.sum(value.astype(F32), axis=1, keepdims=True).astype(jnp.int32)

    def down_rows(value):
        return jnp.sum(value.astype(F32), axis=0, keepdims=True).astype(jnp.int32)

    def column(matrix, at):
        return across_lanes(jnp.where(lanes == at, matrix, zero))

    def swapped(matrix):
        return jnp.concatenate([matrix[half:], matrix[:half]], axis=0)

    note = notes_ref[...].astype(F32)[:, :, 0, :]
    own, other = note[:, 0], note[:, 1]
    note = jnp.concatenate([jnp.where(place < half, own, other), jnp.where(place < half, other, own)], axis=0)
    turned = jnp.concatenate([note] * (LANES // ncol), axis=0).T.astype(jnp.int32)
    total, total_t = zero, zero
    weights = []
    for m in range(3):
        n_row = turned[m:m + 1, :] + zero
        n_col = column(note.astype(jnp.int32), m)
        off_col = across_lanes(jnp.where(lanes < rows, n_row, zero))
        off_row = down_rows(jnp.where(rows < lanes, n_col + zero, zero))
        pairs = jnp.where(inside, (n_col - ((lanes - off_col) & (ncol - 1)) + ncol - 1) // ncol, zero)
        pairs_t = jnp.where(inside, (n_row - ((rows - off_row) & (ncol - 1)) + ncol - 1) // ncol, zero)
        weights.append((off_col, total, column(total_t, place)))
        total, total_t = total + pairs, total_t + pairs_t
    over_t = jnp.maximum(total_t - MAIN, 0)
    over = jnp.maximum(total - MAIN, 0)
    most = jnp.max((total + swapped(total)).astype(F32)) > 2 * MAIN
    many = jnp.max(across_lanes(over).astype(F32)) > HAND
    misfit_ref[0] = (most | many).astype(jnp.int32)

    def ranks(device):
        count = column(over_t, device)
        row = down_rows(jnp.where(rows == device, over, zero))
        rank = lanes - across_lanes(jnp.where(lanes < rows, row + zero, zero))
        return rank, (rank >= 0) & (rank < count)

    rest = ncol * (MAIN + EXTRA)
    rank, hit = ranks(place)
    hand_ref[...] = rest + down_rows(jnp.where(hit, ncol * MAIN + rows * EXTRA + rank - rest, zero))
    rank, hit = ranks(neighbour)
    slot = column(total_t, place) + rank
    insert_ref[...] = down_rows(jnp.where(hit & (slot < MAIN), rows * MAIN + slot + 1, zero)) - 1
    helped = column(swapped(total), place)
    for m, (off_col, ahead, ahead_t) in enumerate(weights):
        start = down_rows(jnp.where(rows == place, off_col + zero, zero))[:, :1]
        local = local_ref[m:m + 1, :]
        owner = (start + local) & (ncol - 1)
        tall = lax.broadcasted_iota(jnp.int32, (ncol, local.shape[1]), 0)
        slot = down_rows(jnp.where(tall == owner, ahead_t, jnp.zeros_like(tall))) + local // ncol
        at = jnp.where(slot < MAIN, owner * MAIN + slot, ncol * MAIN + owner * EXTRA + slot - MAIN)
        send_ref[m:m + 1, :] = jnp.where(local < 0, rest, at)
        wanted = lax.broadcasted_iota(jnp.int32, (1, LANES), 1) * ncol + place
        source = down_rows((off_col <= wanted).astype(jnp.int32)) - 1
        here = rows == source
        start = down_rows(jnp.where(here, off_col, zero))
        slot = down_rows(jnp.where(here, column(ahead, place), zero)) + (wanted - start) // ncol
        used = down_rows(jnp.where(here, helped, zero))
        near = source * MAIN + slot
        helper = (source + half) & (ncol - 1)
        shared_ref[m:m + 1, :] = jnp.where(slot < MAIN, near, helper * MAIN + used + slot - MAIN)
        direct_ref[m:m + 1, :] = jnp.where(slot < MAIN, near, ncol * MAIN + source * EXTRA + slot - MAIN)


def index_tables(place, noted, local, feat, ncol):
    chips, planes, rows, _ = noted.shape
    smem = pl.BlockSpec(memory_space=pltpu.SMEM)
    vmem = pl.BlockSpec(memory_space=pltpu.VMEM)
    wide = jax.ShapeDtypeStruct((1, LANES), jnp.int32)
    three = jax.ShapeDtypeStruct((8, LANES), jnp.int32)
    return pl.pallas_call(
        functools.partial(index_kernel, ncol),
        grid=(1,),
        out_shape=(jax.ShapeDtypeStruct(local.shape, jnp.int32), wide, wide, three, three, jax.ShapeDtypeStruct((1,), jnp.int32)),
        in_specs=[smem, pl.BlockSpec((chips, planes, rows, LANES), lambda i: (0, 0, 0, feat // LANES)), vmem],
        out_specs=(vmem,) * 5 + (smem,),
    )(place.astype(jnp.int32).reshape(1), noted, local)


def shards(tokens, cotangent, gate_weight, up_weight, down_weight, kept, regrown):
    feat, hid = gate_weight.shape
    brows, bcols = kept.shape[1], kept.shape[2]
    ncol = lax.axis_size("col")
    place = lax.axis_index("col")
    core = jnp.stack([lax.axis_index("row") % 2, place // (ncol // 2)]).astype(jnp.int32)
    own = brows * bcols // 4
    rows = tokens.shape[0]
    active = kept + regrown
    tally = jnp.sum(active, axis=(1, 2))
    note = jnp.zeros((rows, LANES), BF).at[0, :3].set(tally.astype(BF))
    go = jnp.sum(tally) >= 0

    x_all = lax.all_to_all(copies(tokens, ncol), "col", 0, 0, tiled=True)
    both, wd = mask_weights(kept, gate_weight, up_weight, down_weight)
    mine = jnp.concatenate([cotangent, note], axis=1)
    joint = jnp.concatenate([mine, across(mine, ncol)], axis=0)
    flat = active.reshape(3, -1)
    local = jnp.where(flat > 0, jnp.cumsum(flat, axis=1) - 1, -1)
    local = jnp.pad(local, ((0, 5), (0, -flat.shape[1] % LANES)), constant_values=-1)
    x_all, both, wd, late, local = tie(x_all, both, wd, copies(joint, ncol // 2), local)
    dy_all = plane_exchange(late, ncol)

    def forward(x_all, both, wd):
        gate_up = row_sum(*shares(core, x_all, both, rows))
        gate, up = gate_up[:, :hid], gate_up[:, hid:]
        hidden = (gate * jax.nn.sigmoid(gate) * up).astype(BF)
        return gate_up, hidden_stage(core, hidden, swap_cores(hidden), wd)

    def backward(local, dy_all, gate_up, both, wd):
        tables = index_tables(place, dy_all.reshape(ncol // 2, 2, rows, -1), local, feat, ncol)
        gate_up_other = swap_cores(gate_up)
        back = row_sum(*shares(core, dy_all, wd, 0))
        done = grads_stage(core, (gate_up, gate_up_other), (back, swap_cores(back)), both)
        return done, tables

    def blocks(send_at, hand_at, insert_at, misfit, x_all, dy_all, grads, hidden):
        misfit = jnp.maximum(misfit, swap_cores(misfit))
        misfit = jnp.maximum(misfit, swap_far(misfit))[0]
        factor = float(rows * ncol) ** (-0.5)
        spread = x_all.reshape(2, ncol // 2, rows, feat)
        main, extra, hand = pack_grads(core, send_at, hand_at, spread, dy_all, grads, hidden, factor, brows, bcols, ncol)
        return insert_blocks(insert_at, across(hand, ncol), main), extra, misfit

    gate_up, (hidden, out_part) = together(go, forward, x_all, both, wd)
    dy_all, gate_up, out_part = tie(dy_all, gate_up, out_part)
    got_out = plane_exchange(out_part, ncol)
    (grads, in_part), (send_at, hand_at, insert_at, shared, direct, misfit) = together(
        go, backward, local, dy_all, gate_up, both, wd)
    got_out, in_part = tie(got_out, in_part)
    got_in = plane_exchange(in_part, ncol)
    main, extra, misfit = together(go, blocks, send_at, hand_at, insert_at, misfit, x_all, dy_all, grads, hidden)
    output = add_parts(got_out, ncol)
    got_in, main, extra, output, misfit = tie(got_in, main, extra, output, misfit)
    got = lax.all_to_all(main, "col", 0, 0, tiled=True)
    input_grad = add_parts(got_in, ncol)

    def with_extra():
        more = lax.all_to_all(extra, "col", 0, 0, tiled=True)
        return pick_blocks(direct, jnp.concatenate([got, more], axis=0), own)

    def without():
        return pick_blocks(shared, got, own)

    grad_blocks = lax.cond(misfit > 0, with_extra, without)
    return (output, input_grad, grad_blocks.reshape(3, 1, 1, own, BLOCK, BLOCK))


def solution(mesh):
    return jax.shard_map(
        shards,
        mesh=mesh,
        in_specs=(
            P("col", "row"),
            P("col", "row"),
            P("row", "col"),
            P("row", "col"),
            P("col", "row"),
            P(None, "row", "col"),
            P(None, "row", "col"),
        ),
        out_specs=(P("col", "row"), P("col", "row"), P(None, "row", "col", None, None, None)),
        check_vma=False,
    )
```

```python
import functools

import jax
import jax.numpy as jnp
from jax import lax
from jax.experimental import pallas as pl
from jax.experimental.pallas import tpu as pltpu
from jax.sharding import PartitionSpec as P

BLOCK = 128
MAIN = 6
EXTRA = 3
HAND = 16
LANES = 128
BF = jnp.bfloat16
F32 = jnp.float32


def contract_last(left, right):
    return lax.dot_general(left, right, (((1,), (1,)), ((), ())), preferred_element_type=F32)


def together(go, step, *args):
    shapes = jax.eval_shape(step, *args)
    return lax.cond(go, step, lambda *_: jax.tree.map(lambda v: jnp.zeros(v.shape, v.dtype), shapes), *args)


def plane_groups(ncol):
    return [list(range(ncol // 2)), list(range(ncol // 2, ncol))]


def across(value, ncol):
    return lax.ppermute(value, "col", [(i, (i + ncol // 2) % ncol) for i in range(ncol)])


def copies(part, many):
    return jnp.broadcast_to(part[None], (many,) + part.shape).reshape(many * part.shape[0], part.shape[1])


def plane_exchange(value, ncol):
    return lax.all_to_all(value, "col", 0, 0, axis_index_groups=plane_groups(ncol), tiled=True)


def add_parts(parts, ncol):
    many = ncol // 2
    sums = [jnp.sum(got.reshape(many, got.shape[0] // many, -1).astype(F32), axis=0) for got in parts]
    rows = sums[0].shape[0] // 2
    came = across(jnp.concatenate([total[rows:].astype(BF) for total in sums], axis=0), ncol).astype(F32)
    return [(total[:rows] + came[i * rows:(i + 1) * rows]).astype(BF) for i, total in enumerate(sums)]


def tie(*values):
    return lax.optimization_barrier(values)


def swap_cores(value):
    return lax.ppermute(value, "row", [(0, 1), (1, 0), (2, 3), (3, 2)])


def swap_far(value):
    return lax.ppermute(value, "row", [(0, 2), (1, 3), (2, 0), (3, 1)])


def row_sum(keep, send):
    mine = keep + swap_cores(send)
    return mine + swap_far(mine.astype(BF)).astype(F32)


def mask_kernel(bcols, kept_ref, gate_ref, up_ref, down_ref, both_ref, out_ref):
    i = pl.program_id(0)
    count = pl.num_programs(0) * bcols
    for f in range(bcols):
        cut = slice(f * BLOCK, (f + 1) * BLOCK)
        for which, from_ref in ((0, gate_ref), (1, up_ref)):
            keep = kept_ref[which * count + i * bcols + f] > 0
            value = from_ref[:, cut]
            both_ref[:, (which * bcols + f) * BLOCK:(which * bcols + f + 1) * BLOCK] = jnp.where(keep, value, jnp.zeros_like(value))
        keep = kept_ref[2 * count + i * bcols + f] > 0
        value = down_ref[cut, :]
        out_ref[cut, :] = jnp.where(keep, value, jnp.zeros_like(value))


def mask_weights(kept, gate, up, down):
    feat, hid = gate.shape
    bcols = hid // BLOCK
    side = pl.BlockSpec((BLOCK, hid), lambda i: (i, 0))
    flat = pl.BlockSpec((hid, BLOCK), lambda i: (0, i))
    return pl.pallas_call(
        functools.partial(mask_kernel, bcols),
        grid=(feat // BLOCK,),
        out_shape=(jax.ShapeDtypeStruct((feat, 2 * hid), BF), jax.ShapeDtypeStruct((hid, feat), BF)),
        in_specs=[pl.BlockSpec(memory_space=pltpu.SMEM), side, side, flat],
        out_specs=(pl.BlockSpec((BLOCK, 2 * hid), lambda i: (i, 0)), flat),
        compiler_params=pltpu.CompilerParams(vmem_limit_bytes=16 * 2**20),
    )(kept.reshape(-1), gate, up, down)


def shares_kernel(reorder, core_ref, rows_ref, weight_ref, keep_ref, send_ref):
    half = keep_ref.shape[0]
    if reorder:
        value = jnp.dot(rows_ref[...], weight_ref[...], preferred_element_type=F32)
    else:
        value = contract_last(rows_ref[:, :weight_ref.shape[1]], weight_ref[...])

    def put(out_ref, which):
        if not reorder:
            out_ref[...] = value[which * half:(which + 1) * half]
            return
        rows = reorder
        chips = 2 * half // rows // 2
        for chip in range(chips // 2):
            for plane in range(2):
                other = jnp.where(core_ref[1] == plane, 0, 1)
                at = pl.multiple_of(2 * chip * rows + other * rows, rows)
                start = (plane * chips + which * chips // 2 + chip) * rows
                out_ref[pl.ds(at, rows), :] = value[start:start + rows]

    @pl.when(core_ref[0] == 0)
    def _():
        put(keep_ref, 0)
        put(send_ref, 1)

    @pl.when(core_ref[0] != 0)
    def _():
        put(keep_ref, 1)
        put(send_ref, 0)


def shares(core, rows, weight, reorder):
    cut = 256
    if reorder:
        feat, wide = weight.shape
        part = pl.BlockSpec((feat, cut), lambda i: (0, i))
    else:
        wide, feat = weight.shape
        part = pl.BlockSpec((cut, feat), lambda i: (i, 0))
    shape = jax.ShapeDtypeStruct((rows.shape[0] // 2, wide), F32)
    out = pl.BlockSpec((rows.shape[0] // 2, cut), lambda i: (0, i))
    return pl.pallas_call(
        functools.partial(shares_kernel, reorder),
        grid=(wide // cut,),
        out_shape=(shape, shape),
        in_specs=[pl.BlockSpec(memory_space=pltpu.SMEM), pl.BlockSpec(memory_space=pltpu.VMEM), part],
        out_specs=(out, out),
        compiler_params=pltpu.CompilerParams(vmem_limit_bytes=40 * 2**20),
    )(core, rows, weight)


def hidden_kernel(core_ref, mine_ref, other_ref, down_ref, hidden_ref, part_ref):
    half = mine_ref.shape[0]

    @pl.when(pl.program_id(0) == 0)
    def _():
        place = pl.multiple_of(core_ref[0] * half, half)
        hidden_ref[pl.ds(place, half), :] = mine_ref[...]
        hidden_ref[pl.ds(pl.multiple_of(half - place, half), half), :] = other_ref[...]

    part_ref[...] = jnp.dot(hidden_ref[...], down_ref[...], preferred_element_type=F32).astype(BF)


def hidden_stage(core, mine, other, wd):
    hid, feat = wd.shape
    cut = 512
    rows = 2 * mine.shape[0]
    vmem = pl.BlockSpec(memory_space=pltpu.VMEM)
    return pl.pallas_call(
        hidden_kernel,
        grid=(feat // cut,),
        out_shape=(jax.ShapeDtypeStruct((rows, hid), BF), jax.ShapeDtypeStruct((rows, feat), BF)),
        in_specs=[pl.BlockSpec(memory_space=pltpu.SMEM), vmem, vmem, pl.BlockSpec((hid, cut), lambda i: (0, i))],
        out_specs=(pl.BlockSpec((rows, hid), lambda i: (0, 0)), pl.BlockSpec((rows, cut), lambda i: (0, i))),
        compiler_params=pltpu.CompilerParams(vmem_limit_bytes=40 * 2**20),
    )(core, mine, other, wd)


def grads_kernel(core_ref, mine_ref, other_ref, back_ref, back_other_ref, both_ref, grads_ref, part_ref):
    half, hid = back_ref.shape

    def point(sums_ref, hidden_grad_ref, at):
        gate, up, hidden_grad = sums_ref[:, :hid], sums_ref[:, hid:], hidden_grad_ref[...]
        sig = jax.nn.sigmoid(gate)
        rows = pl.ds(at, half)
        grads_ref[rows, :hid] = (hidden_grad * up * sig * (1.0 + gate * (1.0 - sig))).astype(BF)
        grads_ref[rows, hid:] = (hidden_grad * (gate * sig)).astype(BF)

    @pl.when(pl.program_id(0) == 0)
    def _():
        place = pl.multiple_of(core_ref[0] * half, half)
        point(mine_ref, back_ref, place)
        point(other_ref, back_other_ref, pl.multiple_of(half - place, half))

    part_ref[...] = contract_last(grads_ref[...], both_ref[...]).astype(BF)


def grads_stage(core, sums, back, both):
    feat, wide = both.shape
    cut = 1024
    rows = 2 * back[0].shape[0]
    vmem = pl.BlockSpec(memory_space=pltpu.VMEM)
    return pl.pallas_call(
        grads_kernel,
        grid=(feat // cut,),
        out_shape=(jax.ShapeDtypeStruct((rows, wide), BF), jax.ShapeDtypeStruct((rows, feat), BF)),
        in_specs=[pl.BlockSpec(memory_space=pltpu.SMEM)] + [vmem] * 4 + [pl.BlockSpec((cut, wide), lambda i: (i, 0))],
        out_specs=(pl.BlockSpec((rows, wide), lambda i: (0, 0)), pl.BlockSpec((rows, cut), lambda i: (0, i))),
        compiler_params=pltpu.CompilerParams(vmem_limit_bytes=44 * 2**20),
    )(core, *sums, *back, both)


def dot_rows(left, right):
    return lax.dot_general(left, right, (((0,), (0,)), ((), ())), preferred_element_type=F32)


def pack_kernel(factor, brows, bcols, group, core_ref, where_ref, hand_at_ref, x_ref, dy_ref, grads_ref, hidden_ref, main_ref, extra_ref, hand_ref, turned_ref, slots_ref, sems):
    cut = main_ref.shape[0]
    more = extra_ref.shape[0]
    wide = group * BLOCK

    def store(which, d, f, block):
        slots_ref[where_ref[which, d * bcols + f]] = block

    turned_ref[...] = hidden_ref[...].T

    def step(i, carry):
        lanes = pl.ds(pl.multiple_of(i * wide, wide), wide)
        planes = (core_ref[1], 1 - core_ref[1])
        x = jnp.concatenate([x_ref[plane, chip, :, lanes] for chip in range(x_ref.shape[1]) for plane in planes], axis=0)
        tile = (dot_rows(x, grads_ref[...]) * factor).astype(BF)
        for which in (0, 1):
            for u in range(group):
                for f in range(bcols):
                    at = (which * bcols + f) * BLOCK
                    store(which, i * group + u, f, tile[u * BLOCK:(u + 1) * BLOCK, at:at + BLOCK])
        tile = (jnp.dot(turned_ref[...], dy_ref[:, lanes], preferred_element_type=F32) * factor).astype(BF)
        for u in range(group):
            for f in range(bcols):
                store(2, i * group + u, f, tile[f * BLOCK:(f + 1) * BLOCK, u * BLOCK:(u + 1) * BLOCK])
        return carry

    lax.fori_loop(0, brows // group, step, 0)
    first = pltpu.make_async_copy(slots_ref.at[pl.ds(0, cut)], main_ref, sems.at[0])
    second = pltpu.make_async_copy(slots_ref.at[pl.ds(cut, more)], extra_ref, sems.at[1])
    first.start()
    second.start()
    for t in range(HAND):
        hand_ref[t] = slots_ref[hand_at_ref[0, t]]
    first.wait()
    second.wait()


def pack_grads(core, where, hand_at, x_all, dy_all, grads, hidden, factor, brows, bcols, ncol):
    vmem = pl.BlockSpec(memory_space=pltpu.VMEM)
    smem = pl.BlockSpec(memory_space=pltpu.SMEM)
    far = pl.BlockSpec(memory_space=pl.ANY)
    return pl.pallas_call(
        functools.partial(pack_kernel, factor, brows, bcols, 4),
        out_shape=tuple(jax.ShapeDtypeStruct((n, BLOCK, BLOCK), BF) for n in (ncol * MAIN, ncol * EXTRA, HAND)),
        in_specs=[smem] * 3 + [vmem] * 4,
        out_specs=(far, far, vmem),
        scratch_shapes=[
            pltpu.VMEM((hidden.shape[1], hidden.shape[0]), BF),
            pltpu.VMEM((ncol * (MAIN + EXTRA) + 1, BLOCK, BLOCK), BF),
            pltpu.SemaphoreType.DMA((2,)),
        ],
        compiler_params=pltpu.CompilerParams(vmem_limit_bytes=48 * 2**20),
    )(core, where, hand_at, x_all, dy_all, grads, hidden)


def insert_kernel(at_ref, got_ref, old_ref, main_ref, spare_ref, sem):
    for t in range(HAND):
        at = at_ref[0, t]

        @pl.when(at >= 0)
        def _():
            pltpu.make_async_copy(got_ref.at[t], main_ref.at[at], sem).start()

        @pl.when(at < 0)
        def _():
            pltpu.make_async_copy(got_ref.at[t], spare_ref.at[t], sem).start()

    pltpu.make_async_copy(got_ref, spare_ref, sem).wait()


def insert_blocks(at, got, main):
    far = pl.BlockSpec(memory_space=pl.ANY)
    return pl.pallas_call(
        insert_kernel,
        out_shape=jax.ShapeDtypeStruct(main.shape, main.dtype),
        in_specs=[pl.BlockSpec(memory_space=pltpu.SMEM), far, far],
        out_specs=far,
        scratch_shapes=[pltpu.VMEM((HAND, BLOCK, BLOCK), BF), pltpu.SemaphoreType.DMA],
        input_output_aliases={2: 0},
    )(at, got, main)


def pick_kernel(own, from_ref, got_ref, out_ref, sem):
    def start(i, carry):
        for m in range(3):
            pltpu.make_async_copy(got_ref.at[from_ref[m, i]], out_ref.at[m * own + i], sem).start()
        return carry

    lax.fori_loop(0, own, start, 0)
    pltpu.make_async_copy(got_ref.at[pl.ds(0, 3 * own)], out_ref, sem).wait()


def pick_blocks(source, got, own):
    return pl.pallas_call(
        functools.partial(pick_kernel, own),
        out_shape=jax.ShapeDtypeStruct((3 * own, BLOCK, BLOCK), BF),
        in_specs=[pl.BlockSpec(memory_space=pltpu.SMEM), pl.BlockSpec(memory_space=pl.ANY)],
        out_specs=pl.BlockSpec(memory_space=pl.ANY),
        scratch_shapes=[pltpu.SemaphoreType.DMA],
    )(source, got)


def index_kernel(ncol, place_ref, notes_ref, local_ref, send_ref, hand_ref, insert_ref, shared_ref, direct_ref, misfit_ref):
    place = place_ref[0]
    half = ncol // 2
    neighbour = (place + half) % ncol
    rows = lax.broadcasted_iota(jnp.int32, (ncol, LANES), 0)
    lanes = lax.broadcasted_iota(jnp.int32, (ncol, LANES), 1)
    inside = lanes < ncol
    zero = jnp.zeros((ncol, LANES), jnp.int32)

    def across_lanes(value):
        return jnp.sum(value.astype(F32), axis=1, keepdims=True).astype(jnp.int32)

    def down_rows(value):
        return jnp.sum(value.astype(F32), axis=0, keepdims=True).astype(jnp.int32)

    def column(matrix, at):
        return across_lanes(jnp.where(lanes == at, matrix, zero))

    def swapped(matrix):
        return jnp.concatenate([matrix[half:], matrix[:half]], axis=0)

    note = notes_ref[...].astype(F32)[:, :, 0, :]
    own, other = note[:, 0], note[:, 1]
    note = jnp.concatenate([jnp.where(place < half, own, other), jnp.where(place < half, other, own)], axis=0)
    turned = jnp.concatenate([note] * (LANES // ncol), axis=0).T.astype(jnp.int32)
    total, total_t = zero, zero
    weights = []
    for m in range(3):
        n_row = turned[m:m + 1, :] + zero
        n_col = column(note.astype(jnp.int32), m)
        off_col = across_lanes(jnp.where(lanes < rows, n_row, zero))
        off_row = down_rows(jnp.where(rows < lanes, n_col + zero, zero))
        pairs = jnp.where(inside, (n_col - ((lanes - off_col) & (ncol - 1)) + ncol - 1) // ncol, zero)
        pairs_t = jnp.where(inside, (n_row - ((rows - off_row) & (ncol - 1)) + ncol - 1) // ncol, zero)
        weights.append((off_col, total, column(total_t, place)))
        total, total_t = total + pairs, total_t + pairs_t
    over_t = jnp.maximum(total_t - MAIN, 0)
    over = jnp.maximum(total - MAIN, 0)
    most = jnp.max((total + swapped(total)).astype(F32)) > 2 * MAIN
    many = jnp.max(across_lanes(over).astype(F32)) > HAND
    misfit_ref[0] = (most | many).astype(jnp.int32)

    def ranks(device):
        count = column(over_t, device)
        row = down_rows(jnp.where(rows == device, over, zero))
        rank = lanes - across_lanes(jnp.where(lanes < rows, row + zero, zero))
        return rank, (rank >= 0) & (rank < count)

    rest = ncol * (MAIN + EXTRA)
    rank, hit = ranks(place)
    hand_ref[...] = rest + down_rows(jnp.where(hit, ncol * MAIN + rows * EXTRA + rank - rest, zero))
    rank, hit = ranks(neighbour)
    slot = column(total_t, place) + rank
    insert_ref[...] = down_rows(jnp.where(hit & (slot < MAIN), rows * MAIN + slot + 1, zero)) - 1
    helped = column(swapped(total), place)
    for m, (off_col, ahead, ahead_t) in enumerate(weights):
        start = down_rows(jnp.where(rows == place, off_col + zero, zero))[:, :1]
        local = local_ref[m:m + 1, :]
        owner = (start + local) & (ncol - 1)
        tall = lax.broadcasted_iota(jnp.int32, (ncol, local.shape[1]), 0)
        slot = down_rows(jnp.where(tall == owner, ahead_t, jnp.zeros_like(tall))) + local // ncol
        at = jnp.where(slot < MAIN, owner * MAIN + slot, ncol * MAIN + owner * EXTRA + slot - MAIN)
        send_ref[m:m + 1, :] = jnp.where(local < 0, rest, at)
        wanted = lax.broadcasted_iota(jnp.int32, (1, LANES), 1) * ncol + place
        source = down_rows((off_col <= wanted).astype(jnp.int32)) - 1
        here = rows == source
        start = down_rows(jnp.where(here, off_col, zero))
        slot = down_rows(jnp.where(here, column(ahead, place), zero)) + (wanted - start) // ncol
        used = down_rows(jnp.where(here, helped, zero))
        near = source * MAIN + slot
        helper = (source + half) & (ncol - 1)
        shared_ref[m:m + 1, :] = jnp.where(slot < MAIN, near, helper * MAIN + used + slot - MAIN)
        direct_ref[m:m + 1, :] = jnp.where(slot < MAIN, near, ncol * MAIN + source * EXTRA + slot - MAIN)


def index_tables(place, noted, local, feat, ncol):
    chips, planes, rows, _ = noted.shape
    smem = pl.BlockSpec(memory_space=pltpu.SMEM)
    vmem = pl.BlockSpec(memory_space=pltpu.VMEM)
    wide = jax.ShapeDtypeStruct((1, LANES), jnp.int32)
    three = jax.ShapeDtypeStruct((8, LANES), jnp.int32)
    return pl.pallas_call(
        functools.partial(index_kernel, ncol),
        grid=(1,),
        out_shape=(jax.ShapeDtypeStruct(local.shape, jnp.int32), wide, wide, three, three, jax.ShapeDtypeStruct((1,), jnp.int32)),
        in_specs=[smem, pl.BlockSpec((chips, planes, rows, LANES), lambda i: (0, 0, 0, feat // LANES)), vmem],
        out_specs=(vmem,) * 5 + (smem,),
    )(place.astype(jnp.int32).reshape(1), noted, local)


def shards(tokens, cotangent, gate_weight, up_weight, down_weight, kept, regrown):
    feat, hid = gate_weight.shape
    brows, bcols = kept.shape[1], kept.shape[2]
    ncol = lax.axis_size("col")
    place = lax.axis_index("col")
    core = jnp.stack([lax.axis_index("row") % 2, place // (ncol // 2)]).astype(jnp.int32)
    own = brows * bcols // 4
    rows = tokens.shape[0]
    active = kept + regrown
    tally = jnp.sum(active, axis=(1, 2))
    note = jnp.zeros((rows, LANES), BF).at[0, :3].set(tally.astype(BF))
    go = jnp.sum(tally) >= 0

    x_all = lax.all_to_all(copies(tokens, ncol), "col", 0, 0, tiled=True)
    both, wd = mask_weights(kept, gate_weight, up_weight, down_weight)
    mine = jnp.concatenate([cotangent, note], axis=1)
    joint = jnp.concatenate([mine, across(mine, ncol)], axis=0)
    flat = active.reshape(3, -1)
    local = jnp.where(flat > 0, jnp.cumsum(flat, axis=1) - 1, -1)
    local = jnp.pad(local, ((0, 5), (0, -flat.shape[1] % LANES)), constant_values=-1)
    x_all, both, wd, late, local = tie(x_all, both, wd, copies(joint, ncol // 2), local)
    dy_all = plane_exchange(late, ncol)

    def forward(x_all, both, wd):
        gate_up = row_sum(*shares(core, x_all, both, rows))
        gate, up = gate_up[:, :hid], gate_up[:, hid:]
        hidden = (gate * jax.nn.sigmoid(gate) * up).astype(BF)
        return gate_up, hidden_stage(core, hidden, swap_cores(hidden), wd)

    def backward(local, dy_all, gate_up, both, wd):
        tables = index_tables(place, dy_all.reshape(ncol // 2, 2, rows, -1), local, feat, ncol)
        gate_up_other = swap_cores(gate_up)
        back = row_sum(*shares(core, dy_all, wd, 0))
        done = grads_stage(core, (gate_up, gate_up_other), (back, swap_cores(back)), both)
        return done, tables

    def blocks(send_at, hand_at, insert_at, misfit, x_all, dy_all, grads, hidden):
        misfit = jnp.maximum(misfit, swap_cores(misfit))
        misfit = jnp.maximum(misfit, swap_far(misfit))[0]
        factor = float(rows * ncol) ** (-0.5)
        spread = x_all.reshape(2, ncol // 2, rows, feat)
        main, extra, hand = pack_grads(core, send_at, hand_at, spread, dy_all, grads, hidden, factor, brows, bcols, ncol)
        return insert_blocks(insert_at, across(hand, ncol), main), extra, misfit

    gate_up, (hidden, out_part) = together(go, forward, x_all, both, wd)
    dy_all, gate_up, out_part = tie(dy_all, gate_up, out_part)
    got_out = plane_exchange(out_part, ncol)
    (grads, in_part), (send_at, hand_at, insert_at, shared, direct, misfit) = together(
        go, backward, local, dy_all, gate_up, both, wd)
    got_out, in_part = tie(got_out, in_part)
    got_in = plane_exchange(in_part, ncol)
    main, extra, misfit = together(go, blocks, send_at, hand_at, insert_at, misfit, x_all, dy_all, grads, hidden)
    got_in, main, extra, got_out, misfit = tie(got_in, main, extra, got_out, misfit)
    got = lax.all_to_all(main, "col", 0, 0, tiled=True)
    output, input_grad = add_parts([got_out, got_in], ncol)

    def with_extra():
        more = lax.all_to_all(extra, "col", 0, 0, tiled=True)
        return pick_blocks(direct, jnp.concatenate([got, more], axis=0), own)

    def without():
        return pick_blocks(shared, got, own)

    grad_blocks = lax.cond(misfit > 0, with_extra, without)
    return (output, input_grad, grad_blocks.reshape(3, 1, 1, own, BLOCK, BLOCK))


def solution(mesh):
    return jax.shard_map(
        shards,
        mesh=mesh,
        in_specs=(
            P("col", "row"),
            P("col", "row"),
            P("row", "col"),
            P("row", "col"),
            P("col", "row"),
            P(None, "row", "col"),
            P(None, "row", "col"),
        ),
        out_specs=(P("col", "row"), P("col", "row"), P(None, "row", "col", None, None, None)),
        check_vma=False,
    )
```

```python
import functools

import jax
import jax.numpy as jnp
from jax import lax
from jax.experimental import pallas as pl
from jax.experimental.pallas import tpu as pltpu
from jax.sharding import PartitionSpec as P

BLOCK = 128
MAIN = 6
EXTRA = 3
HAND = 16
LANES = 128
BF = jnp.bfloat16
F32 = jnp.float32


def contract_last(left, right):
    return lax.dot_general(left, right, (((1,), (1,)), ((), ())), preferred_element_type=F32)


def together(go, step, *args):
    shapes = jax.eval_shape(step, *args)
    return lax.cond(go, step, lambda *_: jax.tree.map(lambda v: jnp.zeros(v.shape, v.dtype), shapes), *args)


def plane_groups(ncol):
    return [list(range(ncol // 2)), list(range(ncol // 2, ncol))]


def across(value, ncol):
    return lax.ppermute(value, "col", [(i, (i + ncol // 2) % ncol) for i in range(ncol)])


def copies(part, many):
    return jnp.broadcast_to(part[None], (many,) + part.shape).reshape(many * part.shape[0], part.shape[1])


def plane_exchange(value, ncol):
    return lax.all_to_all(value, "col", 0, 0, axis_index_groups=plane_groups(ncol), tiled=True)


def add_parts(got, ncol):
    many = ncol // 2
    total = jnp.sum(got.reshape(many, got.shape[0] // many, -1).astype(F32), axis=0)
    rows = total.shape[0] // 2
    return (total[:rows] + across(total[rows:], ncol)).astype(BF)


def tie(*values):
    return lax.optimization_barrier(values)


def swap_cores(value):
    return lax.ppermute(value, "row", [(0, 1), (1, 0), (2, 3), (3, 2)])


def swap_far(value):
    return lax.ppermute(value, "row", [(0, 2), (1, 3), (2, 0), (3, 1)])


def row_parts(keep, send):
    mine = keep + swap_cores(send)
    return mine, swap_far(mine.astype(BF))


def row_sum(mine, far):
    return mine + far.astype(F32)


def mask_kernel(bcols, kept_ref, gate_ref, up_ref, down_ref, both_ref, out_ref):
    i = pl.program_id(0)
    count = pl.num_programs(0) * bcols
    for f in range(bcols):
        cut = slice(f * BLOCK, (f + 1) * BLOCK)
        for which, from_ref in ((0, gate_ref), (1, up_ref)):
            keep = kept_ref[which * count + i * bcols + f] > 0
            value = from_ref[:, cut]
            both_ref[:, (which * bcols + f) * BLOCK:(which * bcols + f + 1) * BLOCK] = jnp.where(keep, value, jnp.zeros_like(value))
        keep = kept_ref[2 * count + i * bcols + f] > 0
        value = down_ref[cut, :]
        out_ref[cut, :] = jnp.where(keep, value, jnp.zeros_like(value))


def mask_weights(kept, gate, up, down):
    feat, hid = gate.shape
    bcols = hid // BLOCK
    side = pl.BlockSpec((BLOCK, hid), lambda i: (i, 0))
    flat = pl.BlockSpec((hid, BLOCK), lambda i: (0, i))
    return pl.pallas_call(
        functools.partial(mask_kernel, bcols),
        grid=(feat // BLOCK,),
        out_shape=(jax.ShapeDtypeStruct((feat, 2 * hid), BF), jax.ShapeDtypeStruct((hid, feat), BF)),
        in_specs=[pl.BlockSpec(memory_space=pltpu.SMEM), side, side, flat],
        out_specs=(pl.BlockSpec((BLOCK, 2 * hid), lambda i: (i, 0)), flat),
        compiler_params=pltpu.CompilerParams(vmem_limit_bytes=16 * 2**20),
    )(kept.reshape(-1), gate, up, down)


def shares_kernel(reorder, core_ref, rows_ref, weight_ref, keep_ref, send_ref):
    half = keep_ref.shape[0]
    if reorder:
        value = jnp.dot(rows_ref[...], weight_ref[...], preferred_element_type=F32)
    else:
        value = contract_last(rows_ref[:, :weight_ref.shape[1]], weight_ref[...])

    def put(out_ref, which):
        if not reorder:
            out_ref[...] = value[which * half:(which + 1) * half]
            return
        rows = reorder
        chips = 2 * half // rows // 2
        for chip in range(chips // 2):
            for plane in range(2):
                other = jnp.where(core_ref[1] == plane, 0, 1)
                at = pl.multiple_of(2 * chip * rows + other * rows, rows)
                start = (plane * chips + which * chips // 2 + chip) * rows
                out_ref[pl.ds(at, rows), :] = value[start:start + rows]

    @pl.when(core_ref[0] == 0)
    def _():
        put(keep_ref, 0)
        put(send_ref, 1)

    @pl.when(core_ref[0] != 0)
    def _():
        put(keep_ref, 1)
        put(send_ref, 0)


def shares(core, rows, weight, reorder):
    cut = 256
    if reorder:
        feat, wide = weight.shape
        part = pl.BlockSpec((feat, cut), lambda i: (0, i))
    else:
        wide, feat = weight.shape
        part = pl.BlockSpec((cut, feat), lambda i: (i, 0))
    shape = jax.ShapeDtypeStruct((rows.shape[0] // 2, wide), F32)
    out = pl.BlockSpec((rows.shape[0] // 2, cut), lambda i: (0, i))
    return pl.pallas_call(
        functools.partial(shares_kernel, reorder),
        grid=(wide // cut,),
        out_shape=(shape, shape),
        in_specs=[pl.BlockSpec(memory_space=pltpu.SMEM), pl.BlockSpec(memory_space=pltpu.VMEM), part],
        out_specs=(out, out),
        compiler_params=pltpu.CompilerParams(vmem_limit_bytes=40 * 2**20),
    )(core, rows, weight)


def hidden_kernel(core_ref, mine_ref, other_ref, down_ref, hidden_ref, part_ref):
    half = mine_ref.shape[0]

    @pl.when(pl.program_id(0) == 0)
    def _():
        place = pl.multiple_of(core_ref[0] * half, half)
        hidden_ref[pl.ds(place, half), :] = mine_ref[...]
        hidden_ref[pl.ds(pl.multiple_of(half - place, half), half), :] = other_ref[...]

    part_ref[...] = jnp.dot(hidden_ref[...], down_ref[...], preferred_element_type=F32).astype(BF)


def hidden_stage(core, mine, other, wd):
    hid, feat = wd.shape
    cut = 512
    rows = 2 * mine.shape[0]
    vmem = pl.BlockSpec(memory_space=pltpu.VMEM)
    return pl.pallas_call(
        hidden_kernel,
        grid=(feat // cut,),
        out_shape=(jax.ShapeDtypeStruct((rows, hid), BF), jax.ShapeDtypeStruct((rows, feat), BF)),
        in_specs=[pl.BlockSpec(memory_space=pltpu.SMEM), vmem, vmem, pl.BlockSpec((hid, cut), lambda i: (0, i))],
        out_specs=(pl.BlockSpec((rows, hid), lambda i: (0, 0)), pl.BlockSpec((rows, cut), lambda i: (0, i))),
        compiler_params=pltpu.CompilerParams(vmem_limit_bytes=40 * 2**20),
    )(core, mine, other, wd)


def grads_kernel(core_ref, mine_ref, other_ref, back_ref, back_other_ref, both_ref, grads_ref, part_ref):
    half, hid = back_ref.shape

    def point(sums_ref, hidden_grad_ref, at):
        gate, up, hidden_grad = sums_ref[:, :hid], sums_ref[:, hid:], hidden_grad_ref[...]
        sig = jax.nn.sigmoid(gate)
        rows = pl.ds(at, half)
        grads_ref[rows, :hid] = (hidden_grad * up * sig * (1.0 + gate * (1.0 - sig))).astype(BF)
        grads_ref[rows, hid:] = (hidden_grad * (gate * sig)).astype(BF)

    @pl.when(pl.program_id(0) == 0)
    def _():
        place = pl.multiple_of(core_ref[0] * half, half)
        point(mine_ref, back_ref, place)
        point(other_ref, back_other_ref, pl.multiple_of(half - place, half))

    part_ref[...] = contract_last(grads_ref[...], both_ref[...]).astype(BF)


def grads_stage(core, sums, back, both):
    feat, wide = both.shape
    cut = 1024
    rows = 2 * back[0].shape[0]
    vmem = pl.BlockSpec(memory_space=pltpu.VMEM)
    return pl.pallas_call(
        grads_kernel,
        grid=(feat // cut,),
        out_shape=(jax.ShapeDtypeStruct((rows, wide), BF), jax.ShapeDtypeStruct((rows, feat), BF)),
        in_specs=[pl.BlockSpec(memory_space=pltpu.SMEM)] + [vmem] * 4 + [pl.BlockSpec((cut, wide), lambda i: (i, 0))],
        out_specs=(pl.BlockSpec((rows, wide), lambda i: (0, 0)), pl.BlockSpec((rows, cut), lambda i: (0, i))),
        compiler_params=pltpu.CompilerParams(vmem_limit_bytes=44 * 2**20),
    )(core, *sums, *back, both)


def dot_rows(left, right):
    return lax.dot_general(left, right, (((0,), (0,)), ((), ())), preferred_element_type=F32)


def pack_kernel(factor, brows, bcols, group, core_ref, where_ref, hand_at_ref, x_ref, dy_ref, grads_ref, hidden_ref, main_ref, extra_ref, hand_ref, turned_ref, slots_ref, sems):
    cut = main_ref.shape[0]
    more = extra_ref.shape[0]
    wide = group * BLOCK

    def store(which, d, f, block):
        slots_ref[where_ref[which, d * bcols + f]] = block

    turned_ref[...] = hidden_ref[...].T

    def step(i, carry):
        lanes = pl.ds(pl.multiple_of(i * wide, wide), wide)
        planes = (core_ref[1], 1 - core_ref[1])
        x = jnp.concatenate([x_ref[plane, chip, :, lanes] for chip in range(x_ref.shape[1]) for plane in planes], axis=0)
        tile = (dot_rows(x, grads_ref[...]) * factor).astype(BF)
        for which in (0, 1):
            for u in range(group):
                for f in range(bcols):
                    at = (which * bcols + f) * BLOCK
                    store(which, i * group + u, f, tile[u * BLOCK:(u + 1) * BLOCK, at:at + BLOCK])
        tile = (jnp.dot(turned_ref[...], dy_ref[:, lanes], preferred_element_type=F32) * factor).astype(BF)
        for u in range(group):
            for f in range(bcols):
                store(2, i * group + u, f, tile[f * BLOCK:(f + 1) * BLOCK, u * BLOCK:(u + 1) * BLOCK])
        return carry

    lax.fori_loop(0, brows // group, step, 0)
    first = pltpu.make_async_copy(slots_ref.at[pl.ds(0, cut)], main_ref, sems.at[0])
    second = pltpu.make_async_copy(slots_ref.at[pl.ds(cut, more)], extra_ref, sems.at[1])
    first.start()
    second.start()
    for t in range(HAND):
        hand_ref[t] = slots_ref[hand_at_ref[0, t]]
    first.wait()
    second.wait()


def pack_grads(core, where, hand_at, x_all, dy_all, grads, hidden, factor, brows, bcols, ncol):
    vmem = pl.BlockSpec(memory_space=pltpu.VMEM)
    smem = pl.BlockSpec(memory_space=pltpu.SMEM)
    far = pl.BlockSpec(memory_space=pl.ANY)
    return pl.pallas_call(
        functools.partial(pack_kernel, factor, brows, bcols, 4),
        out_shape=tuple(jax.ShapeDtypeStruct((n, BLOCK, BLOCK), BF) for n in (ncol * MAIN, ncol * EXTRA, HAND)),
        in_specs=[smem] * 3 + [vmem] * 4,
        out_specs=(far, far, vmem),
        scratch_shapes=[
            pltpu.VMEM((hidden.shape[1], hidden.shape[0]), BF),
            pltpu.VMEM((ncol * (MAIN + EXTRA) + 1, BLOCK, BLOCK), BF),
            pltpu.SemaphoreType.DMA((2,)),
        ],
        compiler_params=pltpu.CompilerParams(vmem_limit_bytes=48 * 2**20),
    )(core, where, hand_at, x_all, dy_all, grads, hidden)


def insert_kernel(at_ref, got_ref, old_ref, main_ref, spare_ref, sem):
    for t in range(HAND):
        at = at_ref[0, t]

        @pl.when(at >= 0)
        def _():
            pltpu.make_async_copy(got_ref.at[t], main_ref.at[at], sem).start()

        @pl.when(at < 0)
        def _():
            pltpu.make_async_copy(got_ref.at[t], spare_ref.at[t], sem).start()

    pltpu.make_async_copy(got_ref, spare_ref, sem).wait()


def insert_blocks(at, got, main):
    far = pl.BlockSpec(memory_space=pl.ANY)
    return pl.pallas_call(
        insert_kernel,
        out_shape=jax.ShapeDtypeStruct(main.shape, main.dtype),
        in_specs=[pl.BlockSpec(memory_space=pltpu.SMEM), far, far],
        out_specs=far,
        scratch_shapes=[pltpu.VMEM((HAND, BLOCK, BLOCK), BF), pltpu.SemaphoreType.DMA],
        input_output_aliases={2: 0},
    )(at, got, main)


def pick_kernel(own, from_ref, got_ref, out_ref, sem):
    def start(i, carry):
        for m in range(3):
            pltpu.make_async_copy(got_ref.at[from_ref[m, i]], out_ref.at[m * own + i], sem).start()
        return carry

    lax.fori_loop(0, own, start, 0)
    pltpu.make_async_copy(got_ref.at[pl.ds(0, 3 * own)], out_ref, sem).wait()


def pick_blocks(source, got, own):
    return pl.pallas_call(
        functools.partial(pick_kernel, own),
        out_shape=jax.ShapeDtypeStruct((3 * own, BLOCK, BLOCK), BF),
        in_specs=[pl.BlockSpec(memory_space=pltpu.SMEM), pl.BlockSpec(memory_space=pl.ANY)],
        out_specs=pl.BlockSpec(memory_space=pl.ANY),
        scratch_shapes=[pltpu.SemaphoreType.DMA],
    )(source, got)


def index_kernel(ncol, place_ref, notes_ref, local_ref, send_ref, hand_ref, insert_ref, shared_ref, direct_ref, misfit_ref):
    place = place_ref[0]
    half = ncol // 2
    neighbour = (place + half) % ncol
    rows = lax.broadcasted_iota(jnp.int32, (ncol, LANES), 0)
    lanes = lax.broadcasted_iota(jnp.int32, (ncol, LANES), 1)
    inside = lanes < ncol
    zero = jnp.zeros((ncol, LANES), jnp.int32)

    def across_lanes(value):
        return jnp.sum(value.astype(F32), axis=1, keepdims=True).astype(jnp.int32)

    def down_rows(value):
        return jnp.sum(value.astype(F32), axis=0, keepdims=True).astype(jnp.int32)

    def column(matrix, at):
        return across_lanes(jnp.where(lanes == at, matrix, zero))

    def swapped(matrix):
        return jnp.concatenate([matrix[half:], matrix[:half]], axis=0)

    note = notes_ref[...].astype(F32)[:, :, 0, :]
    own, other = note[:, 0], note[:, 1]
    note = jnp.concatenate([jnp.where(place < half, own, other), jnp.where(place < half, other, own)], axis=0)
    turned = jnp.concatenate([note] * (LANES // ncol), axis=0).T.astype(jnp.int32)
    total, total_t = zero, zero
    weights = []
    for m in range(3):
        n_row = turned[m:m + 1, :] + zero
        n_col = column(note.astype(jnp.int32), m)
        off_col = across_lanes(jnp.where(lanes < rows, n_row, zero))
        off_row = down_rows(jnp.where(rows < lanes, n_col + zero, zero))
        pairs = jnp.where(inside, (n_col - ((lanes - off_col) & (ncol - 1)) + ncol - 1) // ncol, zero)
        pairs_t = jnp.where(inside, (n_row - ((rows - off_row) & (ncol - 1)) + ncol - 1) // ncol, zero)
        weights.append((off_col, total, column(total_t, place)))
        total, total_t = total + pairs, total_t + pairs_t
    over_t = jnp.maximum(total_t - MAIN, 0)
    over = jnp.maximum(total - MAIN, 0)
    most = jnp.max((total + swapped(total)).astype(F32)) > 2 * MAIN
    many = jnp.max(across_lanes(over).astype(F32)) > HAND
    misfit_ref[0] = (most | many).astype(jnp.int32)

    def ranks(device):
        count = column(over_t, device)
        row = down_rows(jnp.where(rows == device, over, zero))
        rank = lanes - across_lanes(jnp.where(lanes < rows, row + zero, zero))
        return rank, (rank >= 0) & (rank < count)

    rest = ncol * (MAIN + EXTRA)
    rank, hit = ranks(place)
    hand_ref[...] = rest + down_rows(jnp.where(hit, ncol * MAIN + rows * EXTRA + rank - rest, zero))
    rank, hit = ranks(neighbour)
    slot = column(total_t, place) + rank
    insert_ref[...] = down_rows(jnp.where(hit & (slot < MAIN), rows * MAIN + slot + 1, zero)) - 1
    helped = column(swapped(total), place)
    for m, (off_col, ahead, ahead_t) in enumerate(weights):
        start = down_rows(jnp.where(rows == place, off_col + zero, zero))[:, :1]
        local = local_ref[m:m + 1, :]
        owner = (start + local) & (ncol - 1)
        tall = lax.broadcasted_iota(jnp.int32, (ncol, local.shape[1]), 0)
        slot = down_rows(jnp.where(tall == owner, ahead_t, jnp.zeros_like(tall))) + local // ncol
        at = jnp.where(slot < MAIN, owner * MAIN + slot, ncol * MAIN + owner * EXTRA + slot - MAIN)
        send_ref[m:m + 1, :] = jnp.where(local < 0, rest, at)
        wanted = lax.broadcasted_iota(jnp.int32, (1, LANES), 1) * ncol + place
        source = down_rows((off_col <= wanted).astype(jnp.int32)) - 1
        here = rows == source
        start = down_rows(jnp.where(here, off_col, zero))
        slot = down_rows(jnp.where(here, column(ahead, place), zero)) + (wanted - start) // ncol
        used = down_rows(jnp.where(here, helped, zero))
        near = source * MAIN + slot
        helper = (source + half) & (ncol - 1)
        shared_ref[m:m + 1, :] = jnp.where(slot < MAIN, near, helper * MAIN + used + slot - MAIN)
        direct_ref[m:m + 1, :] = jnp.where(slot < MAIN, near, ncol * MAIN + source * EXTRA + slot - MAIN)


def index_tables(place, noted, local, feat, ncol):
    chips, planes, rows, _ = noted.shape
    smem = pl.BlockSpec(memory_space=pltpu.SMEM)
    vmem = pl.BlockSpec(memory_space=pltpu.VMEM)
    wide = jax.ShapeDtypeStruct((1, LANES), jnp.int32)
    three = jax.ShapeDtypeStruct((8, LANES), jnp.int32)
    return pl.pallas_call(
        functools.partial(index_kernel, ncol),
        grid=(1,),
        out_shape=(jax.ShapeDtypeStruct(local.shape, jnp.int32), wide, wide, three, three, jax.ShapeDtypeStruct((1,), jnp.int32)),
        in_specs=[smem, pl.BlockSpec((chips, planes, rows, LANES), lambda i: (0, 0, 0, feat // LANES)), vmem],
        out_specs=(vmem,) * 5 + (smem,),
    )(place.astype(jnp.int32).reshape(1), noted, local)


def shards(tokens, cotangent, gate_weight, up_weight, down_weight, kept, regrown):
    feat, hid = gate_weight.shape
    brows, bcols = kept.shape[1], kept.shape[2]
    ncol = lax.axis_size("col")
    place = lax.axis_index("col")
    core = jnp.stack([lax.axis_index("row") % 2, place // (ncol // 2)]).astype(jnp.int32)
    own = brows * bcols // 4
    rows = tokens.shape[0]
    active = kept + regrown
    tally = jnp.sum(active, axis=(1, 2))
    note = jnp.zeros((rows, LANES), BF).at[0, :3].set(tally.astype(BF))
    go = jnp.sum(tally) >= 0

    x_all = lax.all_to_all(copies(tokens, ncol), "col", 0, 0, tiled=True)
    both, wd = mask_weights(kept, gate_weight, up_weight, down_weight)
    mine = jnp.concatenate([cotangent, note], axis=1)
    joint = jnp.concatenate([mine, across(mine, ncol)], axis=0)
    flat = active.reshape(3, -1)
    local = jnp.where(flat > 0, jnp.cumsum(flat, axis=1) - 1, -1)
    local = jnp.pad(local, ((0, 5), (0, -flat.shape[1] % LANES)), constant_values=-1)
    x_all, both, wd, late, local = tie(x_all, both, wd, copies(joint, ncol // 2), local)
    dy_all = plane_exchange(late, ncol)

    def forward(x_all, both, wd):
        gate_up_parts = row_parts(*shares(core, x_all, both, rows))
        gate_up = row_sum(*gate_up_parts)
        gate, up = gate_up[:, :hid], gate_up[:, hid:]
        hidden = (gate * jax.nn.sigmoid(gate) * up).astype(BF)
        return gate_up_parts, hidden_stage(core, hidden, swap_cores(hidden), wd)

    def backward(local, dy_all, gate_up_parts, both, wd):
        tables = index_tables(place, dy_all.reshape(ncol // 2, 2, rows, -1), local, feat, ncol)
        gate_up = row_sum(*gate_up_parts)
        gate_up_other = swap_cores(gate_up)
        back = row_sum(*row_parts(*shares(core, dy_all, wd, 0)))
        done = grads_stage(core, (gate_up, gate_up_other), (back, swap_cores(back)), both)
        return done, tables

    def blocks(send_at, hand_at, insert_at, misfit, x_all, dy_all, grads, hidden):
        misfit = jnp.maximum(misfit, swap_cores(misfit))
        misfit = jnp.maximum(misfit, swap_far(misfit))[0]
        factor = float(rows * ncol) ** (-0.5)
        spread = x_all.reshape(2, ncol // 2, rows, feat)
        main, extra, hand = pack_grads(core, send_at, hand_at, spread, dy_all, grads, hidden, factor, brows, bcols, ncol)
        return insert_blocks(insert_at, across(hand, ncol), main), extra, misfit

    gate_up_parts, (hidden, out_part) = together(go, forward, x_all, both, wd)
    dy_all, gate_up_parts, out_part = tie(dy_all, gate_up_parts, out_part)
    got_out = plane_exchange(out_part, ncol)
    (grads, in_part), (send_at, hand_at, insert_at, shared, direct, misfit) = together(
        go, backward, local, dy_all, gate_up_parts, both, wd)
    got_out, in_part = tie(got_out, in_part)
    got_in = plane_exchange(in_part, ncol)
    main, extra, misfit = together(go, blocks, send_at, hand_at, insert_at, misfit, x_all, dy_all, grads, hidden)
    output = add_parts(got_out, ncol)
    got_in, main, extra, output, misfit = tie(got_in, main, extra, output, misfit)
    got = lax.all_to_all(main, "col", 0, 0, tiled=True)
    input_grad = add_parts(got_in, ncol)

    def with_extra():
        more = lax.all_to_all(extra, "col", 0, 0, tiled=True)
        return pick_blocks(direct, jnp.concatenate([got, more], axis=0), own)

    def without():
        return pick_blocks(shared, got, own)

    grad_blocks = lax.cond(misfit > 0, with_extra, without)
    return (output, input_grad, grad_blocks.reshape(3, 1, 1, own, BLOCK, BLOCK))


def solution(mesh):
    return jax.shard_map(
        shards,
        mesh=mesh,
        in_specs=(
            P("col", "row"),
            P("col", "row"),
            P("row", "col"),
            P("row", "col"),
            P("col", "row"),
            P(None, "row", "col"),
            P(None, "row", "col"),
        ),
        out_specs=(P("col", "row"), P("col", "row"), P(None, "row", "col", None, None, None)),
        check_vma=False,
    )
```
